128 devices in a mesh: grp: 4 (over z_lo, core), wide: 32 (over y, x, z_hi).
Axes of the slice: x: 4, y: 4, z: 4 (z_hi: 2, z_lo: 2; z = z_hi * 2 + z_lo), core: 2. Of those that a mesh axis runs over, the one named last changes fastest.
Arguments:
- student_feats: bfloat16 [128, 256, 1280], P(('grp', 'wide')), may hold values from -6 to 6
- dino_in: bfloat16 [128, 256, 1536], P('grp', 'wide'), may hold values from -6 to 6
- siglip_in: bfloat16 [128, 256, 1152], P('grp', 'wide'), may hold values from -6 to 6
- sam_in: bfloat16 [128, 1024, 1280], P('grp', 'wide'), may hold values from -6 to 6
- dino_proj: bfloat16 [1536, 1536], P(None, 'wide'), may hold values from -0.15625 to 0.15625
- siglip_proj: bfloat16 [1152, 1152], P(None, 'wide'), may hold values from -0.1875 to 0.1875
- sam_proj: bfloat16 [1280, 1280], P(None, 'wide'), may hold values from -0.15625 to 0.15625
- dino_index: int32 [128, 256], P(('grp', 'wide')), may hold values from 0 to 255, as said below
- siglip_index: int32 [128, 256], P(('grp', 'wide')), may hold values from 0 to 255, as said below
- sam_index: int32 [128, 256], P(('grp', 'wide')), may hold values from 0 to 255, as said below
- dino_first: bfloat16 [1280, 640], P('wide'), may hold values from -0.15625 to 0.15625
- dino_second: bfloat16 [640, 1536], P('wide'), may hold values from -0.25 to 0.25
- siglip_first: bfloat16 [1280, 640], P('wide'), may hold values from -0.15625 to 0.15625
- siglip_second: bfloat16 [640, 1152], P('wide'), may hold values from -0.25 to 0.25
- sam_first: bfloat16 [1280, 640], P('wide'), may hold values from -0.15625 to 0.15625
- sam_second: bfloat16 [640, 1280], P('wide'), may hold values from -0.25 to 0.25
Outputs:
- dino_first_grad: float32 [1280, 640], P('wide')
- dino_second_grad: float32 [640, 1536], P('wide')
- siglip_first_grad: float32 [1280, 640], P('wide')
- siglip_second_grad: float32 [640, 1152], P('wide')
- sam_first_grad: float32 [1280, 640], P('wide')
- sam_second_grad: float32 [640, 1280], P('wide')
The draws below stay inside these ranges and needn't reach their ends.
Inputs may be any that keep to these rules, and one draw needn't show every extreme that they name: dino_index[i, s] is the cell of the 16 x 16 grid under student patch s of image i, after that image's optional left-right mirror. siglip_index[i, s] is the cell of the 16 x 16 grid under student patch s of image i, after that image's optional left-right mirror. sam_index[i, s] is the block of the 16 x 16 grid of SAM blocks under student patch s of image i, after that image's optional left-right mirror.
All inputs are finite; a program needn't handle non-finite values.
Results may differ from the reference program's by a relative error of at most 0.002.
Values may be sent and summed in bfloat16 or wider, within the bound.
A program may use at most 128 MiB of HBM per device.

```python
import math
import jax
import jax.numpy as jnp
from jax import lax

D = 1280
HID = 640
WD = 1536
WS = 1152
WM = 1280
SIDE = 16
GRID_D = 16
GRID_S = 16
GRID_M = 32
PATCHES = 256
CELLS_D = 256
CELLS_S = 256
CELLS_M = 1024
IMAGES = 128


def grid_cells(key, grid):
    key_flip, key_row, key_col = jax.random.split(key, 3)
    ratio = grid // SIDE
    flips = jax.random.randint(key_flip, (IMAGES, 1), 0, 2)
    shift_row = jax.random.randint(key_row, (IMAGES, 1), 0, ratio)
    shift_col = jax.random.randint(key_col, (IMAGES, 1), 0, ratio)
    image_number = jnp.arange(IMAGES, dtype=jnp.int32)[:, None]
    flips = jnp.where(image_number == 0, 1, jnp.where(image_number == 1, 0, flips))
    shift_row = jnp.where(image_number == 0, ratio - 1, jnp.where(image_number == 1, 0, shift_row))
    shift_col = jnp.where(image_number < 2, 0, shift_col)
    patch = jnp.arange(PATCHES, dtype=jnp.int32)[None, :]
    cell_row = patch // SIDE * ratio + shift_row
    cell_col = patch % SIDE * ratio + shift_col
    cell_col = jnp.where(flips == 1, grid - 1 - cell_col, cell_col)
    return (cell_row * grid + cell_col).astype(jnp.int32)


def draw_dino_index(key, part):
    key = jax.random.fold_in(key, 11)
    return grid_cells(key, GRID_D)


def draw_siglip_index(key, part):
    key = jax.random.fold_in(key, 23)
    return grid_cells(key, GRID_S)


def draw_sam_index(key, part):
    key = jax.random.fold_in(key, 37)
    return grid_cells(key, SIDE)


def levels(stream_key, dims, pieces, least, largest):
    level = 1.0
    for position, shards_of in pieces:
        heights = jax.random.uniform(jax.random.fold_in(jax.random.fold_in(stream_key, 6), position), (shards_of,), jnp.float32, least / len(pieces), largest / len(pieces))
        level = level * jnp.repeat(jnp.exp(heights), dims[position] // shards_of).reshape((-1,) + (1,) * (len(dims) - 1 - position))
    return level


def bell_draw(key, extent, spread, reach, cuts=(), held_as=jnp.bfloat16):
    values = jax.random.normal(key, extent, jnp.float32) * spread
    if len(cuts) > 0:
        values = levels(key, extent, cuts, -0.22, 0.18) * values
    return jnp.clip(values, min=-reach, max=reach).astype(held_as)


def setup_inputs(seed: int = 0) -> dict:
    key_list = jax.random.split(jax.random.key(seed), 17)
    student_feats = bell_draw(key_list[0], (IMAGES, PATCHES, D), 1.0, 6.0, ((0, 128),))
    dino_in = bell_draw(key_list[1], (IMAGES, CELLS_D, WD), 1.0, 6.0, ((0, 4), (1, 32)))
    siglip_in = bell_draw(key_list[2], (IMAGES, CELLS_S, WS), 1.0, 6.0, ((0, 4), (1, 32)))
    sam_in = bell_draw(key_list[3], (IMAGES, CELLS_M, WM), 1.0, 6.0, ((0, 4), (1, 32)))
    dino_proj = bell_draw(key_list[4], (WD, WD), WD ** -0.5, 0.15625, ((1, 32),))
    siglip_proj = bell_draw(key_list[5], (WS, WS), WS ** -0.5, 0.1875, ((1, 32),))
    sam_proj = bell_draw(key_list[6], (WM, WM), WM ** -0.5, 0.15625, ((1, 32),))
    dino_index = draw_dino_index(jax.random.fold_in(key_list[16], 71), 0)
    siglip_index = draw_siglip_index(jax.random.fold_in(key_list[16], 71), 0)
    sam_index = draw_sam_index(jax.random.fold_in(key_list[16], 71), 0)
    dino_first = bell_draw(key_list[10], (D, HID), D ** -0.5, 0.15625, ((0, 32),))
    dino_second = bell_draw(key_list[11], (HID, WD), HID ** -0.5, 0.25, ((0, 32),))
    siglip_first = bell_draw(key_list[12], (D, HID), D ** -0.5, 0.15625, ((0, 32),))
    siglip_second = bell_draw(key_list[13], (HID, WS), HID ** -0.5, 0.25, ((0, 32),))
    sam_first = bell_draw(key_list[14], (D, HID), D ** -0.5, 0.15625, ((0, 32),))
    sam_second = bell_draw(key_list[15], (HID, WM), HID ** -0.5, 0.25, ((0, 32),))
    return {"student_feats": student_feats, "dino_in": dino_in, "siglip_in": siglip_in, "sam_in": sam_in, "dino_proj": dino_proj, "siglip_proj": siglip_proj, "sam_proj": sam_proj, "dino_index": dino_index, "siglip_index": siglip_index, "sam_index": sam_index, "dino_first": dino_first, "dino_second": dino_second, "siglip_first": siglip_first, "siglip_second": siglip_second, "sam_first": sam_first, "sam_second": sam_second}


def layer_norm(values):
    centered = values - lax.optimization_barrier(jnp.mean(values, axis=-1, keepdims=True))
    variance = lax.optimization_barrier(jnp.mean(centered * centered, axis=-1, keepdims=True))
    return centered * lax.rsqrt(variance + 1e-05)

def gelu_pair(act):
    cdf = 0.5 * (1.0 + jax.scipy.special.erf(act * (1.0 / math.sqrt(2.0))))
    density = jnp.exp(-0.5 * act * act) * (1.0 / math.sqrt(2.0 * math.pi))
    return (act * cdf, cdf + act * density)

def take_cells(cell_map, cell_index):
    return cell_map[cell_index]

def teacher_target(inputs, projection, index):
    chosen = jax.vmap(take_cells)(inputs, index)
    rows = chosen.reshape(-1, chosen.shape[-1])
    mixed = jnp.dot(rows, projection, preferred_element_type=jnp.float32)
    return layer_norm(rows.astype(jnp.float32) + mixed).astype(jnp.bfloat16)

def sam_target(inputs, projection, index):
    ratio = GRID_M // SIDE
    group_cells = ratio * ratio

    def one_image(image):
        mixed = jnp.dot(image, projection, preferred_element_type=jnp.float32)
        cell_map = layer_norm(image.astype(jnp.float32) + mixed).astype(jnp.bfloat16)
        cell_map = lax.optimization_barrier(cell_map)
        blocks = cell_map.astype(jnp.float32).reshape(-1, group_cells, cell_map.shape[-1])
        return lax.optimization_barrier(jnp.mean(blocks, axis=1)).astype(jnp.bfloat16)
    pooled = lax.map(one_image, inputs)
    chosen = jax.vmap(take_cells)(pooled, index)
    return chosen.reshape(-1, chosen.shape[-1])

def full_total(left, right):
    return lax.dot_general(left, right, (((0,), (0,)), ((), ())), preferred_element_type=jnp.float32)

def teacher_grads(normed, target, first, second):
    act = jnp.dot(normed, first, preferred_element_type=jnp.float32)
    hid_full, slope = gelu_pair(act)
    hidden = hid_full.astype(jnp.bfloat16)
    pred = jnp.dot(hidden, second, preferred_element_type=jnp.float32)
    grad_pred = (2.0 / IMAGES * (pred - target.astype(jnp.float32))).astype(jnp.bfloat16)
    grad_hid = jnp.dot(grad_pred, second.T, preferred_element_type=jnp.float32)
    grad_act = (grad_hid * slope).astype(jnp.bfloat16)
    return (full_total(normed, grad_act), full_total(hidden, grad_pred))

def reference(student_feats, dino_in, siglip_in, sam_in, dino_proj, siglip_proj, sam_proj, dino_index, siglip_index, sam_index, dino_first, dino_second, siglip_first, siglip_second, sam_first, sam_second):
    normed = layer_norm(student_feats.reshape(-1, D).astype(jnp.float32)).astype(jnp.bfloat16)
    dino_target = teacher_target(dino_in, dino_proj, dino_index)
    siglip_target = teacher_target(siglip_in, siglip_proj, siglip_index)
    sam_rows = sam_target(sam_in, sam_proj, sam_index)
    dino_one, dino_two = teacher_grads(normed, dino_target, dino_first, dino_second)
    siglip_one, siglip_two = teacher_grads(normed, siglip_target, siglip_first, siglip_second)
    sam_one, sam_two = teacher_grads(normed, sam_rows, sam_first, sam_second)
    return (dino_one, dino_two, siglip_one, siglip_two, sam_one, sam_two)
```

```python
import functools
import itertools
import math

import jax
import jax.numpy as jnp
from jax import lax
from jax.experimental import pallas as pl
from jax.experimental.pallas import tpu as pltpu
from jax.sharding import PartitionSpec as P

MESH = pl.DeviceIdType.MESH
LANE = 128
ALL = (0, 4)
BOTH = (0, 2)


def layer_norm(values, count=None, mask=None):
    count = values.shape[-1] if count is None else count
    centered = values - jnp.sum(values, axis=-1, keepdims=True) * (1.0 / count)
    if mask is not None:
        centered = centered * mask
    variance = jnp.sum(centered * centered, axis=-1, keepdims=True) * (1.0 / count)
    return centered * lax.rsqrt(variance + 1e-05)


def gelu_pair(act):
    cdf = 0.5 * (1.0 + jax.scipy.special.erf(act * (1.0 / math.sqrt(2.0))))
    density = jnp.exp(-0.5 * act * act) * (1.0 / math.sqrt(2.0 * math.pi))
    return (act * cdf, cdf + act * density)


class Place:
    def __init__(self):
        grp, wide = lax.axis_index("grp"), lax.axis_index("wide")
        self.grp, self.wide = grp, wide
        self.z_lo, self.core = grp // 2, grp % 2
        self.y, self.x, self.z_hi = wide // 8, wide // 2 % 4, wide % 2

    def x_next(self, step):
        return (self.grp, (self.y * 4 + self.x_at(step)) * 2 + self.z_hi)

    def y_next(self, step):
        return (self.grp, (self.y_at(step) * 4 + self.x) * 2 + self.z_hi)

    def x_at(self, step):
        return (self.x + step + 4) % 4

    def y_at(self, step):
        return (self.y + step + 4) % 4

    def mirror_z(self):
        return ((1 - self.z_lo) * 2 + self.core, (self.y * 4 + self.x) * 2 + 1 - self.z_hi)

    def next_z(self):
        return ((1 - self.z_lo) * 2 + self.core, self.wide)

    def sibling(self):
        return (self.z_lo * 2 + 1 - self.core, self.wide)


def enter(partners):
    barrier = pltpu.get_barrier_semaphore()
    for partner in partners:
        pl.semaphore_signal(barrier, inc=1, device_id=partner, device_id_type=MESH)
    pl.semaphore_wait(barrier, len(partners))


def part(entry):
    return pl.ds(entry[0], entry[1]) if isinstance(entry, tuple) else entry


def extent(entry):
    return entry[1] if isinstance(entry, tuple) else None


class Copies:
    def __init__(self, send_sem, recv_sem):
        self.numbers = itertools.count()
        self.send_sem, self.recv_sem = send_sem, recv_sem
        self.started = []

    def send(self, src, dst, device):
        i = next(self.numbers)
        copy = pltpu.make_async_remote_copy(
            src_ref=src,
            dst_ref=dst,
            send_sem=self.send_sem.at[i],
            recv_sem=self.recv_sem.at[i],
            device_id=device,
            device_id_type=MESH,
        )
        copy.start()
        self.started.append(copy)
        return copy

    def finish(self):
        for copy in self.started:
            copy.wait_send()


def take_turns(streams):
    streams = list(streams)
    while streams:
        streams = [stream for stream in streams if next(stream, None) is not None]


def gather_kernel(splits, *refs):
    count = len(splits)
    ins, outs = refs[:count], refs[count : 2 * count]
    local_sem, send_sem, recv_sem = refs[2 * count :]
    at = Place()
    enter(
        [
            at.x_next(1),
            at.x_next(-1),
            at.y_next(1),
            at.y_next(-1),
            at.mirror_z(),
            at.sibling(),
        ]
    )
    copies = Copies(send_sem, recv_sem)
    halves = []

    def lanes(k, s):
        start = at.core * sum(splits[k]) + sum(splits[k][:s])
        return pl.ds(pl.multiple_of(start * LANE, LANE), splits[k][s] * LANE)

    def view(k, s, region):
        return outs[k].at[part(region[0]), part(region[1]), part(region[2]), :, lanes(k, s)]

    own = (at.y, at.x, at.z_hi)
    kept = [
        pltpu.make_async_copy(ins[k], outs[k].at[at.y, at.x, at.z_hi], local_sem.at[k])
        for k in range(count)
    ]
    for copy in kept:
        copy.start()

    def send(s, region, device, ks=None):
        ks = range(count) if ks is None else ks
        return [
            copies.send(
                ins[k].at[:, lanes(k, s)] if region is own else view(k, s, region),
                view(k, s, region),
                device,
            )
            for k in ks
        ]

    def arrived(s, sent, region, ks=None):
        for copy in sent:
            copy.wait_recv()
        halves.extend(send(s, region, at.sibling(), ks))

    def across(s, block):
        sent = send(s, block(at.z_hi), at.mirror_z())
        yield True
        arrived(s, sent, block(1 - at.z_hi))

    def around(s, block, place, device, cut=None):
        up = send(s, block(place(0)), device(1))
        down = send(s, block(place(0)), device(-1))
        yield True
        even, odd = range(0, count, 2), range(1, count, 2)
        arrived(s, up, block(place(-1)))
        if cut is None:
            up = send(s, block(place(-1)), device(1), even)
        else:
            up = send(s, cut(block(place(-1)), 0), device(1))
        arrived(s, down, block(place(1)))
        if cut is None:
            down = send(s, block(place(1)), device(-1), odd)
        else:
            down = send(s, cut(block(place(1)), 1), device(-1))
        yield True
        if cut is None:
            arrived(s, up, block(place(2)), even)
            arrived(s, down, block(place(2)), odd)
        else:
            arrived(s, up, cut(block(place(2)), 0))
            arrived(s, down, cut(block(place(2)), 1))

    def cut_y(region, half):
        return ((half * 2, 2), region[1], region[2])

    def cut_x(region, half):
        return (region[0], (half * 2, 2), region[2])

    def cut_z(region, half):
        return (region[0], region[1], half)

    def first_stream():
        yield from across(0, lambda c: own if c is at.z_hi else (at.y, at.x, c))
        yield from around(0, lambda c: (c, at.x, BOTH), at.y_at, at.y_next, cut_z)
        yield from around(0, lambda c: (ALL, c, BOTH), at.x_at, at.x_next, cut_y)

    def second_stream():
        yield from around(1, lambda c: (at.y, c, at.z_hi), at.x_at, at.x_next)
        yield from across(1, lambda c: (at.y, ALL, c))
        yield from around(1, lambda c: (c, ALL, BOTH), at.y_at, at.y_next, cut_x)

    def third_stream():
        yield from around(2, lambda c: (c, at.x, at.z_hi), at.y_at, at.y_next)
        yield from around(2, lambda c: (ALL, c, at.z_hi), at.x_at, at.x_next, cut_y)
        yield from across(2, lambda c: (ALL, ALL, c))

    for copy in kept:
        copy.wait()
    take_turns([first_stream(), second_stream(), third_stream()])
    for copy in halves:
        copy.wait_recv()
    copies.finish()


def gather(shards, splits):
    outs = [jax.ShapeDtypeStruct((4, 4, 2) + shard.shape, shard.dtype) for shard in shards]
    whole = pl.BlockSpec(memory_space=pl.ANY)
    semaphores = pltpu.SemaphoreType.DMA((52 * len(shards),))
    gathered = pl.pallas_call(
        functools.partial(gather_kernel, splits),
        out_shape=outs,
        in_specs=[whole] * len(shards),
        out_specs=[whole] * len(shards),
        scratch_shapes=[pltpu.SemaphoreType.DMA((len(shards),)), semaphores, semaphores],
        compiler_params=pltpu.CompilerParams(collective_id=0, has_side_effects=True),
        name="gather_weights",
    )(*shards)
    return [g.reshape(-1, g.shape[-1]) for g in gathered]


def reduce_kernel(splits, *refs):
    count = len(splits)
    ins, outs = refs[:count], refs[count : 2 * count]
    sums, last = refs[2 * count : 3 * count], refs[3 * count : 4 * count]
    spare, (send_sem, recv_sem) = refs[4 * count : -2], refs[-2:]
    at = Place()
    enter(
        [
            at.x_next(1),
            at.x_next(-1),
            at.y_next(1),
            at.y_next(-1),
            at.mirror_z(),
            at.next_z(),
            at.sibling(),
        ]
    )
    copies = Copies(send_sem, recv_sem)
    numbers = itertools.count()

    def lanes(k, s):
        return pl.ds(sum(splits[k][:s]) * LANE, splits[k][s] * LANE)

    def wide_lanes(k, s, core):
        start = core * sum(splits[k]) + sum(splits[k][:s])
        return pl.ds(pl.multiple_of(start * LANE, LANE), splits[k][s] * LANE)

    def view(k, s, region):
        return sums[k].at[part(region[0]), part(region[1]), part(region[2]), :, lanes(k, s)]

    def send(s, region, device, ks=None):
        sent = []
        for k in range(count) if ks is None else ks:
            room = spare[next(numbers)]
            sent.append((k, room, copies.send(view(k, s, region), room, device)))
        return sent

    def add(s, sent, region):
        for k, room, copy in sent:
            copy.wait_recv()
            sizes = [extent(entry) for entry in region]
            steps = [size or 1 for size in sizes]

            @pl.loop(0, steps[0] * steps[1] * steps[2])
            def _(i, k=k, room=room, sizes=sizes, steps=steps):
                spots = (i // (steps[1] * steps[2]), i // steps[2] % steps[1], i % steps[2])
                there = tuple(spot for spot, size in zip(spots, sizes) if size)
                here = tuple(
                    spot + entry[0] if size else entry
                    for spot, size, entry in zip(spots, sizes, region)
                )
                where = here + (slice(None), lanes(k, s))
                sums[k][where] = sums[k][where] + room[there + (slice(None), slice(None))]

    def across(s, block):
        sent = send(s, block(1 - at.z_hi), at.mirror_z())
        yield True
        add(s, sent, block(at.z_hi))

    def around(s, block, place, device, cut=None):
        even, odd = range(0, count, 2), range(1, count, 2)
        if cut is None:
            up = send(s, block(place(2)), device(1), even)
            down = send(s, block(place(2)), device(-1), odd)
        else:
            up = send(s, cut(block(place(2)), 0), device(1))
            down = send(s, cut(block(place(2)), 1), device(-1))
        yield True
        add(s, up, block(place(1)) if cut is None else cut(block(place(1)), 0))
        up = send(s, block(place(1)), device(1))
        add(s, down, block(place(-1)) if cut is None else cut(block(place(-1)), 1))
        down = send(s, block(place(-1)), device(-1))
        yield True
        add(s, up, block(place(0)))
        add(s, down, block(place(0)))

    def cut_y(region, half):
        return ((half * 2, 2), region[1], region[2])

    def cut_x(region, half):
        return (region[0], (half * 2, 2), region[2])

    def cut_z(region, half):
        return (region[0], region[1], half)

    chip = [
        [
            copies.send(
                ins[k].at[:, :, :, :, wide_lanes(k, s, 1 - at.core)],
                sums[k].at[:, :, :, :, lanes(k, s)],
                at.sibling(),
            )
            for k in range(count)
        ]
        for s in range(3)
    ]

    def join(s):
        for k in range(count):
            chip[s][k].wait_recv()

            @pl.loop(0, 32)
            def _(i, k=k):
                spot = (i // 8, i // 2 % 4, i % 2, slice(None))
                mine = ins[k][spot + (wide_lanes(k, s, at.core),)]
                sums[k][spot + (lanes(k, s),)] = sums[k][spot + (lanes(k, s),)] + mine

    def first_stream():
        join(0)
        yield from around(0, lambda c: (ALL, c, BOTH), at.x_at, at.x_next, cut_y)
        yield from around(0, lambda c: (c, at.x, BOTH), at.y_at, at.y_next, cut_z)
        yield from across(0, lambda c: (at.y, at.x, c))

    def second_stream():
        join(1)
        yield from around(1, lambda c: (c, ALL, BOTH), at.y_at, at.y_next, cut_x)
        yield from across(1, lambda c: (at.y, ALL, c))
        yield from around(1, lambda c: (at.y, c, at.z_hi), at.x_at, at.x_next)

    def third_stream():
        join(2)
        yield from across(2, lambda c: (ALL, ALL, c))
        yield from around(2, lambda c: (ALL, c, at.z_hi), at.x_at, at.x_next, cut_y)
        yield from around(2, lambda c: (c, at.x, at.z_hi), at.y_at, at.y_next)

    take_turns([first_stream(), second_stream(), third_stream()])
    own = (at.y, at.x, at.z_hi)
    pairs = [copies.send(sums[k].at[own], last[k], at.next_z()) for k in range(count)]
    halves = []
    for k in range(count):
        pairs[k].wait_recv()
        outs[k][at.core] = sums[k][own] + last[k][...]
        halves.append(copies.send(outs[k].at[at.core], outs[k].at[at.core], at.sibling()))
    for copy in halves:
        copy.wait_recv()
    copies.finish()


def spare_shapes(rows, splits):
    count = len(rows)

    def room(k, s, lead):
        return pltpu.VMEM(lead + (rows[k], splits[k][s] * LANE), jnp.float32)

    def across(s, lead):
        yield [room(k, s, lead) for k in range(count)]

    def around(s, lead, half=None):
        if half is None:
            yield [room(k, s, lead) for k in range(0, count, 2)] + [
                room(k, s, lead) for k in range(1, count, 2)
            ]
        else:
            yield [room(k, s, half) for k in range(count)] * 2
        yield [room(k, s, lead) for k in range(count)] * 2

    streams = [
        itertools.chain(around(0, (4, 2), (2, 2)), around(0, (2,), ()), across(0, ())),
        itertools.chain(around(1, (4, 2), (2, 2)), across(1, (4,)), around(1, ())),
        itertools.chain(across(2, (4, 4)), around(2, (4,), (2,)), around(2, ())),
    ]
    shapes = []
    while streams:
        left = []
        for stream in streams:
            group = next(stream, None)
            if group is not None:
                shapes.extend(group)
                left.append(stream)
        streams = left
    return shapes


def reduce_sum(partials, splits):
    count = len(partials)
    rows = [p.shape[-2] for p in partials]
    width = [p.shape[-1] // 2 for p in partials]
    inside = pl.BlockSpec(memory_space=pltpu.VMEM)
    semaphores = pltpu.SemaphoreType.DMA((32 * count,))
    out = pl.pallas_call(
        functools.partial(reduce_kernel, splits),
        out_shape=[
            jax.ShapeDtypeStruct((2, r, w), jnp.float32) for r, w in zip(rows, width)
        ],
        in_specs=[inside] * count,
        out_specs=[inside] * count,
        scratch_shapes=[pltpu.VMEM((4, 4, 2, r, w), jnp.float32) for r, w in zip(rows, width)]
        + [pltpu.VMEM((r, w), jnp.float32) for r, w in zip(rows, width)]
        + spare_shapes(rows, splits)
        + [semaphores, semaphores],
        compiler_params=pltpu.CompilerParams(
            collective_id=1, has_side_effects=True, vmem_limit_bytes=62 * 1024 * 1024
        ),
        name="reduce_gradients",
    )(*partials)
    return [jnp.concatenate([o[0], o[1]], axis=-1) for o in out]


def spread(width, group, room):
    rows = lax.broadcasted_iota(jnp.int32, (width, width // group * room), 0)
    columns = lax.broadcasted_iota(jnp.int32, (width, width // group * room), 1)
    return (rows // group * room + rows % group == columns).astype(jnp.bfloat16)


def place_columns(values, table):
    return jnp.dot(values, table, preferred_element_type=jnp.float32).astype(jnp.bfloat16)


def teacher_map(rows, projection, count=None, mask=None):
    mixed = lax.dot_general(
        rows, projection, (((1,), (1,)), ((), ())), preferred_element_type=jnp.float32
    )
    return layer_norm(rows.astype(jnp.float32) + mixed, count, mask).astype(jnp.bfloat16)


def pool_blocks(maps):
    held = lax.optimization_barrier(maps)
    blocks = held.astype(jnp.float32).reshape(maps.shape[0] // 4, 4, maps.shape[1])
    return jnp.mean(blocks, axis=1).astype(jnp.bfloat16)


def adaptor_grads(normed, target, first, second, factor):
    act = jnp.dot(normed, first, preferred_element_type=jnp.float32)
    hid_full, slope = gelu_pair(act)
    hidden = hid_full.astype(jnp.bfloat16)
    pred = jnp.dot(hidden, second, preferred_element_type=jnp.float32)
    grad_pred = (factor * (pred - target.astype(jnp.float32))).astype(jnp.bfloat16)
    grad_hid = lax.dot_general(
        grad_pred, second, (((1,), (1,)), ((), ())), preferred_element_type=jnp.float32
    )
    grad_act = (grad_hid * slope).astype(jnp.bfloat16)
    first_part = lax.dot_general(
        normed, grad_act, (((0,), (0,)), ((), ())), preferred_element_type=jnp.float32
    )
    second_part = lax.dot_general(
        hidden, grad_pred, (((0,), (0,)), ((), ())), preferred_element_type=jnp.float32
    )
    return (first_part, second_part)


def student_rows(student_feats, indices):
    normed = layer_norm(student_feats[0].astype(jnp.float32)).astype(jnp.bfloat16)
    patches = jnp.arange(256, dtype=jnp.int32)
    flags = jnp.stack([index[0] == patches for index in indices], axis=-1).astype(jnp.bfloat16)
    rows = jnp.concatenate([normed, jnp.pad(flags, ((0, 0), (0, LANE - 3)))], axis=-1)
    grid = rows.reshape(16, 16, -1)
    return jnp.concatenate(
        [grid.reshape(32, 8, -1), grid[:, ::-1].reshape(32, 8, -1)], axis=1
    )


def body(
    student_feats,
    dino_in,
    siglip_in,
    sam_in,
    dino_proj,
    siglip_proj,
    sam_proj,
    dino_index,
    siglip_index,
    sam_index,
    dino_first,
    dino_second,
    siglip_first,
    siglip_second,
    sam_first,
    sam_second,
):
    images_total = student_feats.shape[0] * 128
    rows = lax.all_to_all(
        student_rows(student_feats, (dino_index, siglip_index, sam_index)),
        "wide",
        split_axis=0,
        concat_axis=0,
        tiled=True,
    )
    width = student_feats.shape[-1]
    siglip_room = spread(1152, 36, 40)
    hidden_room = spread(640, 20, 24)
    siglip_turned = jnp.pad(place_columns(siglip_proj.T, siglip_room), ((0, 4), (0, 0)))
    firsts = place_columns(
        jnp.concatenate([dino_first, siglip_first, sam_first], axis=0), hidden_room
    ).reshape(3, 40, 768)
    seconds = jnp.concatenate(
        [dino_second, place_columns(siglip_second, siglip_room), sam_second], axis=1
    )
    dino_all, mixed_all, second_all = gather(
        [
            dino_proj.T,
            jnp.concatenate([sam_proj.T, siglip_turned, *firsts], axis=1),
            jnp.pad(seconds, ((0, 4), (0, 0))),
        ],
        ((2, 2, 2), (7, 7, 5), (6, 6, 4)),
    )
    sam_all, siglip_all, first_all = jnp.split(mixed_all, [1280, 2560], axis=1)

    siglip_mask = (jnp.arange(1280) % 40 < 36).astype(jnp.float32)
    targets = (
        teacher_map(dino_in.reshape(256, -1), dino_all),
        teacher_map(
            place_columns(siglip_in.reshape(256, -1), siglip_room), siglip_all, 1152, siglip_mask
        ),
        pool_blocks(teacher_map(sam_in.reshape(1024, -1), sam_all)),
    )
    factor = 2.0 / images_total
    straight, mirrored = rows[:, :8, :width], rows[:, 8:, :width]
    first_parts, second_parts = [], []
    for t, (target, begin, end) in enumerate(
        zip(targets, (0, 1536, 2816), (1536, 2816, 4096))
    ):
        flag = rows[:, :8, width + t : width + t + 1] > 0
        normed = jnp.where(flag, straight, mirrored).reshape(256, width)
        one, two = adaptor_grads(
            normed,
            target,
            first_all[:, t * 768 : (t + 1) * 768],
            second_all[:, begin:end],
            factor,
        )
        first_parts.append(one)
        second_parts.append(two)
    first_sum, second_sum = reduce_sum(
        [
            jnp.concatenate(first_parts, axis=1).reshape(4, 4, 2, 40, 2304),
            jnp.concatenate(second_parts, axis=1).reshape(4, 4, 2, 24, 4096),
        ],
        ((3, 3, 3), (6, 6, 4)),
    )
    firsts = first_sum.reshape(40, 3, 32, 24)[..., :20].reshape(40, 3, 640)
    seconds = second_sum[:20]
    siglip_two = seconds[:, 1536:2816].reshape(20, 32, 40)[..., :36].reshape(20, 1152)
    return (
        firsts[:, 0],
        seconds[:, :1536],
        firsts[:, 1],
        siglip_two,
        firsts[:, 2],
        seconds[:, 2816:],
    )


def solution(mesh):
    shared = P("wide", None)
    return jax.shard_map(
        body,
        mesh=mesh,
        in_specs=(
            P(("grp", "wide"), None, None),
            *[P("grp", "wide", None)] * 3,
            *[P(None, "wide")] * 3,
            *[P(("grp", "wide"), None)] * 3,
            *[shared] * 6,
        ),
        out_specs=(shared,) * 6,
        check_vma=False,
    )
```

```python
import functools
import itertools
import math

import jax
import jax.numpy as jnp
from jax import lax
from jax.experimental import pallas as pl
from jax.experimental.pallas import tpu as pltpu
from jax.sharding import PartitionSpec as P

MESH = pl.DeviceIdType.MESH
LANE = 128
ALL = (0, 4)
BOTH = (0, 2)


def layer_norm(values, count=None, mask=None):
    count = values.shape[-1] if count is None else count
    centered = values - jnp.sum(values, axis=-1, keepdims=True) * (1.0 / count)
    if mask is not None:
        centered = centered * mask
    variance = jnp.sum(centered * centered, axis=-1, keepdims=True) * (1.0 / count)
    return centered * lax.rsqrt(variance + 1e-05)


def gelu_pair(act):
    cdf = 0.5 * (1.0 + jax.scipy.special.erf(act * (1.0 / math.sqrt(2.0))))
    density = jnp.exp(-0.5 * act * act) * (1.0 / math.sqrt(2.0 * math.pi))
    return (act * cdf, cdf + act * density)


class Place:
    def __init__(self):
        grp, wide = lax.axis_index("grp"), lax.axis_index("wide")
        self.grp, self.wide = grp, wide
        self.z_lo, self.core = grp // 2, grp % 2
        self.y, self.x, self.z_hi = wide // 8, wide // 2 % 4, wide % 2

    def x_next(self, step):
        return (self.grp, (self.y * 4 + self.x_at(step)) * 2 + self.z_hi)

    def y_next(self, step):
        return (self.grp, (self.y_at(step) * 4 + self.x) * 2 + self.z_hi)

    def x_at(self, step):
        return (self.x + step + 4) % 4

    def y_at(self, step):
        return (self.y + step + 4) % 4

    def mirror_z(self):
        return ((1 - self.z_lo) * 2 + self.core, (self.y * 4 + self.x) * 2 + 1 - self.z_hi)

    def next_z(self):
        return ((1 - self.z_lo) * 2 + self.core, self.wide)

    def sibling(self):
        return (self.z_lo * 2 + 1 - self.core, self.wide)


def enter(partners):
    barrier = pltpu.get_barrier_semaphore()
    for partner in partners:
        pl.semaphore_signal(barrier, inc=1, device_id=partner, device_id_type=MESH)
    pl.semaphore_wait(barrier, len(partners))


def part(entry):
    return pl.ds(entry[0], entry[1]) if isinstance(entry, tuple) else entry


def extent(entry):
    return entry[1] if isinstance(entry, tuple) else None


class Copies:
    def __init__(self, send_sem, recv_sem):
        self.numbers = itertools.count()
        self.send_sem, self.recv_sem = send_sem, recv_sem
        self.started = []

    def send(self, src, dst, device):
        i = next(self.numbers)
        copy = pltpu.make_async_remote_copy(
            src_ref=src,
            dst_ref=dst,
            send_sem=self.send_sem.at[i],
            recv_sem=self.recv_sem.at[i],
            device_id=device,
            device_id_type=MESH,
        )
        copy.start()
        self.started.append(copy)
        return copy

    def finish(self):
        for copy in self.started:
            copy.wait_send()


class Task:
    def __init__(self, link, cost, needs, run, rank=0):
        self.link, self.cost, self.run, self.rank = link, cost, run, rank
        self.needs = [need for need in needs if need is not None]
        self.copy, self.landed, self.done = None, False, None


def plan(tasks):
    free, now, order, left = {}, 0.0, [], list(tasks)
    while left:
        able = [
            (max([need.done for need in task.needs], default=0.0), task)
            for task in left
            if all(need.done is not None for need in task.needs)
        ]
        soon = [pair for pair in able if pair[0] <= now]
        if soon:
            ready, task = min(soon, key=lambda pair: (pair[1].link == "core", pair[1].rank, pair[0]))
        else:
            ready, task = min(able, key=lambda pair: (pair[0], pair[1].rank))
        now = max(now, ready)
        if task.link == "core":
            now += task.cost
            task.done = now
        else:
            now += 0.15
            rate = {"sibling": 0.4, "local": 0.4}.get(task.link, 0.0445)
            free[task.link] = max(now, free.get(task.link, 0.0)) + task.cost * 1e-6 / rate
            task.done = free[task.link] + 1.5
        order.append(task)
        left.remove(task)
    return order


def carry_out(order):
    for task in order:
        for need in task.needs:
            land(need)
        task.copy = task.run()
    for task in order:
        land(task)


def land(task):
    if task.copy is not None and not task.landed:
        if task.link == "local":
            task.copy.wait()
        else:
            task.copy.wait_recv()
        task.landed = True


def take_turns(streams):
    streams = list(streams)
    while streams:
        streams = [stream for stream in streams if next(stream, None) is not None]


def cut_y(region, half):
    return ((half * 2, 2), region[1], region[2])


def cut_x(region, half):
    return (region[0], (half * 2, 2), region[2])


def cut_z(region, half):
    return (region[0], region[1], half)


def chunks(region):
    return math.prod(extent(entry) or 1 for entry in region)


def gather_kernel(splits, *refs):
    count = len(splits)
    ins, refs = refs[:count], refs[count:]
    (dino_in, siglip_in, sam_in), refs = refs[:3], refs[3:]
    (first_out, second_out, dino_out, siglip_out, sam_out), refs = refs[:5], refs[5:]
    dino_all, mixed_all, pre, cells, local_sem, send_sem, recv_sem = refs
    outs = (dino_all, mixed_all, first_out, second_out)
    at = Place()
    enter(
        [
            at.x_next(1),
            at.x_next(-1),
            at.y_next(1),
            at.y_next(-1),
            at.mirror_z(),
            at.next_z(),
            at.sibling(),
        ]
    )
    copies = Copies(send_sem, recv_sem)
    tasks = []

    def lanes(k, s):
        start = at.core * sum(splits[k]) + sum(splits[k][:s])
        return pl.ds(pl.multiple_of(start * LANE, LANE), splits[k][s] * LANE)

    def view(k, s, region):
        return outs[k].at[part(region[0]), part(region[1]), part(region[2]), :, lanes(k, s)]

    def keep(k):
        def run():
            copy = pltpu.make_async_copy(
                ins[k], outs[k].at[at.y, at.x, at.z_hi], local_sem.at[k]
            )
            copy.start()
            return copy

        return Task("local", ins[k].shape[0] * ins[k].shape[1] * 2, [], run, k)

    kept = [keep(k) for k in range(count)]
    tasks.extend(kept)

    def send(k, s, region, link, device, needs):
        def run():
            src = ins[k].at[:, lanes(k, s)] if region is own else view(k, s, region)
            return copies.send(src, view(k, s, region), device)

        size = chunks(region) * ins[k].shape[0] * splits[k][s] * LANE * 2
        task = Task(link, size, needs, run, k)
        tasks.append(task)
        return task

    own = (at.y, at.x, at.z_hi)
    found = [[] for _ in range(count)]

    def arrive(k, s, region, task):
        half = send(k, s, region, "sibling", at.sibling(), [task])
        found[k] += [task, half]
        return task

    def across(k, s, needs):
        task = send(k, s, own, "mirror", at.mirror_z(), needs)
        return [arrive(k, s, (at.y, at.x, 1 - at.z_hi), task)]

    def across_both(k, s, needs):
        first = send(k, s, ((2 - 2 * at.z_lo, 2), ALL, at.z_hi), "mirror", at.mirror_z(), needs)
        here = ((2 * at.z_lo, 2), ALL, 1 - at.z_hi)
        arrive(k, s, here, first)
        second = send(k, s, here, "next", at.next_z(), [first])
        arrive(k, s, ((2 - 2 * at.z_lo, 2), ALL, 1 - at.z_hi), second)

    def around(k, s, axis, block, cut, needs):
        place, device = (at.x_at, at.x_next) if axis == "x" else (at.y_at, at.y_next)
        here = own if cut is None else block(place(0))
        back, ahead, over = block(place(-1)), block(place(1)), block(place(2))
        up = arrive(k, s, back, send(k, s, here, axis + "+", device(1), needs))
        down = arrive(k, s, ahead, send(k, s, here, axis + "-", device(-1), needs))
        got = [up, down]
        if cut is not None:
            task = send(k, s, cut(back, 0), axis + "+", device(1), [up])
            got.append(arrive(k, s, cut(over, 0), task))
            task = send(k, s, cut(ahead, 1), axis + "-", device(-1), [down])
            got.append(arrive(k, s, cut(over, 1), task))
        elif k % 2 == 0:
            task = send(k, s, back, axis + "+", device(1), [up])
            got.append(arrive(k, s, over, task))
        else:
            task = send(k, s, ahead, axis + "-", device(-1), [down])
            got.append(arrive(k, s, over, task))
        return got

    for k in range(count):
        mine = [kept[k]]
        got = across(k, 0, [])
        got = mine + got + around(k, 0, "y", lambda c: (c, at.x, BOTH), cut_z, mine + got)
        around(k, 0, "x", lambda c: (ALL, c, BOTH), cut_y, got)
        got = across(k, 1, [])
        got = mine + got + around(k, 1, "x", lambda c: (at.y, c, BOTH), cut_z, mine + got)
        around(k, 1, "y", lambda c: (c, ALL, BOTH), cut_x, got)
        got = mine + around(k, 2, "x", lambda c: (at.y, c, at.z_hi), None, [])
        got = got + around(k, 2, "y", lambda c: (c, ALL, at.z_hi), cut_x, got)
        across_both(k, 2, got)
        got = mine + around(k, 3, "y", lambda c: (c, at.x, at.z_hi), None, [])
        got = got + around(k, 3, "x", lambda c: (ALL, c, at.z_hi), cut_y, got)
        across_both(k, 3, got)

    def mix(rows_ref, begin, weights, lane, width, count, mask, write):
        rows = rows_ref[begin : begin + 256, :]
        step = weights.shape[3] * 16
        for half in range(2):
            block = weights[2 * half : 2 * half + 2, :, :, :, lane : lane + rows.shape[1]]
            mixed = lax.dot_general(
                rows,
                block.reshape(step, rows.shape[1]),
                (((1,), (1,)), ((), ())),
                preferred_element_type=jnp.float32,
            )
            side = rows[:, half * step : (half + 1) * step].astype(jnp.float32)
            pre[:, half * step : (half + 1) * step] = side + mixed

        @pl.loop(0, 8)
        def _(i):
            spot = pl.ds(pl.multiple_of(i * 32, 32), 32)
            values = pre[spot, :width]
            write(spot, layer_norm(values, count, mask).astype(jnp.bfloat16))

    def dino():
        def write(spot, values):
            dino_out[spot, :] = values

        mix(dino_in, 0, dino_all, 0, 1536, 1536, None, write)

    def siglip():
        def write(spot, values):
            siglip_out[spot, :] = values

        column = lax.broadcasted_iota(jnp.int32, (1, 1280), 1)
        mask = (column % 40 < 36).astype(jnp.float32)
        mix(siglip_in, 0, mixed_all, 1280, 1280, 1152, mask, write)

    def sam(b):
        def run():
            def write(spot, values):
                cells[spot, :] = values

            mix(sam_in, b * 256, mixed_all, 0, 1280, 1280, None, write)
            block = lax.broadcasted_iota(jnp.int32, (64, 256), 0)
            cell = lax.broadcasted_iota(jnp.int32, (64, 256), 1)
            member = ((cell >= 4 * block) & (cell < 4 * block + 4)).astype(jnp.bfloat16)
            total = jnp.dot(member, cells[...], preferred_element_type=jnp.float32)
            sam_out[b * 64 : b * 64 + 64, :] = (total * 0.25).astype(jnp.bfloat16)

        return run

    tasks.append(Task("core", 4.0, found[0] + [kept[0]], dino))
    tasks.append(Task("core", 4.0, found[1] + [kept[1]], siglip))
    for b in range(4):
        tasks.append(Task("core", 3.5, found[1] + [kept[1]], sam(b)))
    carry_out(plan(tasks))
    copies.finish()


def gather_and_map(shards, rows, splits):
    whole = pl.BlockSpec(memory_space=pl.ANY)
    inside = pl.BlockSpec(memory_space=pltpu.VMEM)
    shapes = [(4, 4, 2) + shard.shape for shard in shards]
    semaphores = pltpu.SemaphoreType.DMA((72 * len(shards),))
    first, second, dino, siglip, sam = pl.pallas_call(
        functools.partial(gather_kernel, splits),
        out_shape=[
            jax.ShapeDtypeStruct(shapes[2], jnp.bfloat16),
            jax.ShapeDtypeStruct(shapes[3], jnp.bfloat16),
            jax.ShapeDtypeStruct((256, 1536), jnp.bfloat16),
            jax.ShapeDtypeStruct((256, 1280), jnp.bfloat16),
            jax.ShapeDtypeStruct((256, 1280), jnp.bfloat16),
        ],
        in_specs=[whole] * len(shards) + [inside] * 3,
        out_specs=[whole] * 2 + [inside] * 3,
        scratch_shapes=[
            pltpu.VMEM(shapes[0], jnp.bfloat16),
            pltpu.VMEM(shapes[1], jnp.bfloat16),
            pltpu.VMEM((256, 1536), jnp.float32),
            pltpu.VMEM((256, 1280), jnp.bfloat16),
            pltpu.SemaphoreType.DMA((len(shards),)),
            semaphores,
            semaphores,
        ],
        compiler_params=pltpu.CompilerParams(
            collective_id=0, has_side_effects=True, vmem_limit_bytes=60 * 1024 * 1024
        ),
        name="gather_and_map",
    )(*shards, *rows)
    return [first.reshape(1280, -1), second.reshape(768, -1), dino, siglip, sam]


def reduce_kernel(splits, *refs):
    count = len(splits)
    ins, outs = refs[:count], refs[count : 2 * count]
    sums, last = refs[2 * count : 3 * count], refs[3 * count : 4 * count]
    spare, (send_sem, recv_sem) = refs[4 * count : -2], refs[-2:]
    at = Place()
    enter(
        [
            at.x_next(1),
            at.x_next(-1),
            at.y_next(1),
            at.y_next(-1),
            at.mirror_z(),
            at.next_z(),
            at.sibling(),
        ]
    )
    copies = Copies(send_sem, recv_sem)
    numbers = itertools.count()

    def lanes(k, s):
        return pl.ds(sum(splits[k][:s]) * LANE, splits[k][s] * LANE)

    def wide_lanes(k, s, core):
        start = core * sum(splits[k]) + sum(splits[k][:s])
        return pl.ds(pl.multiple_of(start * LANE, LANE), splits[k][s] * LANE)

    def view(k, s, region):
        return sums[k].at[part(region[0]), part(region[1]), part(region[2]), :, lanes(k, s)]

    def send(s, region, device, ks=None):
        sent = []
        for k in range(count) if ks is None else ks:
            room = spare[next(numbers)]
            sent.append((k, room, copies.send(view(k, s, region), room, device)))
        return sent

    def add(s, sent, region):
        for k, room, copy in sent:
            copy.wait_recv()
            sizes = [extent(entry) for entry in region]
            steps = [size or 1 for size in sizes]

            @pl.loop(0, steps[0] * steps[1] * steps[2])
            def _(i, k=k, room=room, sizes=sizes, steps=steps):
                spots = (i // (steps[1] * steps[2]), i // steps[2] % steps[1], i % steps[2])
                there = tuple(spot for spot, size in zip(spots, sizes) if size)
                here = tuple(
                    spot + entry[0] if size else entry
                    for spot, size, entry in zip(spots, sizes, region)
                )
                where = here + (slice(None), lanes(k, s))
                sums[k][where] = sums[k][where] + room[there + (slice(None), slice(None))]

    def across(s, block):
        sent = send(s, block(1 - at.z_hi), at.mirror_z())
        yield True
        add(s, sent, block(at.z_hi))

    def around(s, block, place, device, cut=None):
        even, odd = range(0, count, 2), range(1, count, 2)
        if cut is None:
            up = send(s, block(place(2)), device(1), even)
            down = send(s, block(place(2)), device(-1), odd)
        else:
            up = send(s, cut(block(place(2)), 0), device(1))
            down = send(s, cut(block(place(2)), 1), device(-1))
        yield True
        add(s, up, block(place(1)) if cut is None else cut(block(place(1)), 0))
        up = send(s, block(place(1)), device(1))
        add(s, down, block(place(-1)) if cut is None else cut(block(place(-1)), 1))
        down = send(s, block(place(-1)), device(-1))
        yield True
        add(s, up, block(place(0)))
        add(s, down, block(place(0)))

    def cut_y(region, half):
        return ((half * 2, 2), region[1], region[2])

    def cut_x(region, half):
        return (region[0], (half * 2, 2), region[2])

    def cut_z(region, half):
        return (region[0], region[1], half)

    chip = [
        [
            copies.send(
                ins[k].at[:, :, :, :, wide_lanes(k, s, 1 - at.core)],
                sums[k].at[:, :, :, :, lanes(k, s)],
                at.sibling(),
            )
            for k in range(count)
        ]
        for s in range(3)
    ]

    def join(s):
        for k in range(count):
            chip[s][k].wait_recv()

            @pl.loop(0, 32)
            def _(i, k=k):
                spot = (i // 8, i // 2 % 4, i % 2, slice(None))
                mine = ins[k][spot + (wide_lanes(k, s, at.core),)]
                sums[k][spot + (lanes(k, s),)] = sums[k][spot + (lanes(k, s),)] + mine

    def first_stream():
        join(0)
        yield from around(0, lambda c: (ALL, c, BOTH), at.x_at, at.x_next, cut_y)
        yield from around(0, lambda c: (c, at.x, BOTH), at.y_at, at.y_next, cut_z)
        yield from across(0, lambda c: (at.y, at.x, c))

    def second_stream():
        join(1)
        yield from around(1, lambda c: (c, ALL, BOTH), at.y_at, at.y_next, cut_x)
        yield from across(1, lambda c: (at.y, ALL, c))
        yield from around(1, lambda c: (at.y, c, at.z_hi), at.x_at, at.x_next)

    def third_stream():
        join(2)
        yield from across(2, lambda c: (ALL, ALL, c))
        yield from around(2, lambda c: (ALL, c, at.z_hi), at.x_at, at.x_next, cut_y)
        yield from around(2, lambda c: (c, at.x, at.z_hi), at.y_at, at.y_next)

    take_turns([first_stream(), second_stream(), third_stream()])
    own = (at.y, at.x, at.z_hi)
    pairs = [copies.send(sums[k].at[own], last[k], at.next_z()) for k in range(count)]
    halves = []
    for k in range(count):
        pairs[k].wait_recv()
        outs[k][at.core] = sums[k][own] + last[k][...]
        halves.append(copies.send(outs[k].at[at.core], outs[k].at[at.core], at.sibling()))
    for copy in halves:
        copy.wait_recv()
    copies.finish()


def spare_shapes(rows, splits):
    count = len(rows)

    def room(k, s, lead):
        return pltpu.VMEM(lead + (rows[k], splits[k][s] * LANE), jnp.float32)

    def across(s, lead):
        yield [room(k, s, lead) for k in range(count)]

    def around(s, lead, half=None):
        if half is None:
            yield [room(k, s, lead) for k in range(0, count, 2)] + [
                room(k, s, lead) for k in range(1, count, 2)
            ]
        else:
            yield [room(k, s, half) for k in range(count)] * 2
        yield [room(k, s, lead) for k in range(count)] * 2

    streams = [
        itertools.chain(around(0, (4, 2), (2, 2)), around(0, (2,), ()), across(0, ())),
        itertools.chain(around(1, (4, 2), (2, 2)), across(1, (4,)), around(1, ())),
        itertools.chain(across(2, (4, 4)), around(2, (4,), (2,)), around(2, ())),
    ]
    shapes = []
    while streams:
        left = []
        for stream in streams:
            group = next(stream, None)
            if group is not None:
                shapes.extend(group)
                left.append(stream)
        streams = left
    return shapes


def reduce_sum(partials, splits):
    count = len(partials)
    rows = [p.shape[-2] for p in partials]
    width = [p.shape[-1] // 2 for p in partials]
    inside = pl.BlockSpec(memory_space=pltpu.VMEM)
    semaphores = pltpu.SemaphoreType.DMA((32 * count,))
    out = pl.pallas_call(
        functools.partial(reduce_kernel, splits),
        out_shape=[
            jax.ShapeDtypeStruct((2, r, w), jnp.float32) for r, w in zip(rows, width)
        ],
        in_specs=[inside] * count,
        out_specs=[inside] * count,
        scratch_shapes=[pltpu.VMEM((4, 4, 2, r, w), jnp.float32) for r, w in zip(rows, width)]
        + [pltpu.VMEM((r, w), jnp.float32) for r, w in zip(rows, width)]
        + spare_shapes(rows, splits)
        + [semaphores, semaphores],
        compiler_params=pltpu.CompilerParams(
            collective_id=1, has_side_effects=True, vmem_limit_bytes=62 * 1024 * 1024
        ),
        name="reduce_gradients",
    )(*partials)
    return [jnp.concatenate([o[0], o[1]], axis=-1) for o in out]


def spread(width, group, room):
    rows = lax.broadcasted_iota(jnp.int32, (width, width // group * room), 0)
    columns = lax.broadcasted_iota(jnp.int32, (width, width // group * room), 1)
    return (rows // group * room + rows % group == columns).astype(jnp.bfloat16)


def place_columns(values, table):
    return jnp.dot(values, table, preferred_element_type=jnp.float32).astype(jnp.bfloat16)


def adaptor_grads(normed, target, first, second, factor):
    act = jnp.dot(normed, first, preferred_element_type=jnp.float32)
    hid_full, slope = gelu_pair(act)
    hidden = hid_full.astype(jnp.bfloat16)
    pred = jnp.dot(hidden, second, preferred_element_type=jnp.float32)
    grad_pred = (factor * (pred - target.astype(jnp.float32))).astype(jnp.bfloat16)
    grad_hid = lax.dot_general(
        grad_pred, second, (((1,), (1,)), ((), ())), preferred_element_type=jnp.float32
    )
    grad_act = (grad_hid * slope).astype(jnp.bfloat16)
    first_part = lax.dot_general(
        normed, grad_act, (((0,), (0,)), ((), ())), preferred_element_type=jnp.float32
    )
    second_part = lax.dot_general(
        hidden, grad_pred, (((0,), (0,)), ((), ())), preferred_element_type=jnp.float32
    )
    return (first_part, second_part)


def student_rows(student_feats, indices):
    normed = layer_norm(student_feats[0].astype(jnp.float32)).astype(jnp.bfloat16)
    patches = jnp.arange(256, dtype=jnp.int32)
    flags = jnp.stack([index[0] == patches for index in indices], axis=-1).astype(jnp.bfloat16)
    rows = jnp.concatenate([normed, jnp.pad(flags, ((0, 0), (0, LANE - 3)))], axis=-1)
    grid = rows.reshape(16, 16, -1)
    return jnp.concatenate(
        [grid.reshape(32, 8, -1), grid[:, ::-1].reshape(32, 8, -1)], axis=1
    )


def body(
    student_feats,
    dino_in,
    siglip_in,
    sam_in,
    dino_proj,
    siglip_proj,
    sam_proj,
    dino_index,
    siglip_index,
    sam_index,
    dino_first,
    dino_second,
    siglip_first,
    siglip_second,
    sam_first,
    sam_second,
):
    images_total = student_feats.shape[0] * 128
    rows = lax.all_to_all(
        student_rows(student_feats, (dino_index, siglip_index, sam_index)),
        "wide",
        split_axis=0,
        concat_axis=0,
        tiled=True,
    )
    width = student_feats.shape[-1]
    siglip_room = spread(1152, 36, 40)
    hidden_room = spread(640, 20, 24)
    siglip_turned = jnp.pad(place_columns(siglip_proj.T, siglip_room), ((0, 4), (0, 0)))
    firsts = place_columns(
        jnp.concatenate([dino_first, siglip_first, sam_first], axis=0), hidden_room
    ).reshape(3, 40, 768)
    seconds = jnp.concatenate(
        [dino_second, place_columns(siglip_second, siglip_room), sam_second], axis=1
    )
    first_all, second_all, *targets = gather_and_map(
        [
            dino_proj.T,
            jnp.concatenate([sam_proj.T, siglip_turned], axis=1),
            jnp.concatenate([*firsts], axis=1),
            jnp.pad(seconds, ((0, 4), (0, 0))),
        ],
        [
            dino_in.reshape(256, -1),
            place_columns(siglip_in.reshape(256, -1), siglip_room),
            sam_in.reshape(1024, -1),
        ],
        ((1, 1, 2, 2), (2, 2, 3, 3), (2, 2, 3, 2), (3, 3, 5, 5)),
    )
    factor = 2.0 / images_total
    straight, mirrored = rows[:, :8, :width], rows[:, 8:, :width]
    first_parts, second_parts = [], []
    for t, (target, begin, end) in enumerate(
        zip(targets, (0, 1536, 2816), (1536, 2816, 4096))
    ):
        flag = rows[:, :8, width + t : width + t + 1] > 0
        normed = jnp.where(flag, straight, mirrored).reshape(256, width)
        one, two = adaptor_grads(
            normed,
            target,
            first_all[:, t * 768 : (t + 1) * 768],
            second_all[:, begin:end],
            factor,
        )
        first_parts.append(one)
        second_parts.append(two)
    first_sum, second_sum = reduce_sum(
        [
            jnp.concatenate(first_parts, axis=1).reshape(4, 4, 2, 40, 2304),
            jnp.concatenate(second_parts, axis=1).reshape(4, 4, 2, 24, 4096),
        ],
        ((3, 3, 3), (6, 6, 4)),
    )
    firsts = first_sum.reshape(40, 3, 32, 24)[..., :20].reshape(40, 3, 640)
    seconds = second_sum[:20]
    siglip_two = seconds[:, 1536:2816].reshape(20, 32, 40)[..., :36].reshape(20, 1152)
    return (
        firsts[:, 0],
        seconds[:, :1536],
        firsts[:, 1],
        siglip_two,
        firsts[:, 2],
        seconds[:, 2816:],
    )


def solution(mesh):
    shared = P("wide", None)
    return jax.shard_map(
        body,
        mesh=mesh,
        in_specs=(
            P(("grp", "wide"), None, None),
            *[P("grp", "wide", None)] * 3,
            *[P(None, "wide")] * 3,
            *[P(("grp", "wide"), None)] * 3,
            *[shared] * 6,
        ),
        out_specs=(shared,) * 6,
        check_vma=False,
    )
```

```python
import functools
import itertools
import math

import jax
import jax.numpy as jnp
from jax import lax
from jax.experimental import pallas as pl
from jax.experimental.pallas import tpu as pltpu
from jax.sharding import PartitionSpec as P

MESH = pl.DeviceIdType.MESH
LANE = 128
ALL = (0, 4)
BOTH = (0, 2)


def layer_norm(values, count=None, mask=None):
    count = values.shape[-1] if count is None else count
    centered = values - jnp.sum(values, axis=-1, keepdims=True) * (1.0 / count)
    if mask is not None:
        centered = centered * mask
    variance = jnp.sum(centered * centered, axis=-1, keepdims=True) * (1.0 / count)
    return centered * lax.rsqrt(variance + 1e-05)


def gelu_pair(act):
    cdf = 0.5 * (1.0 + jax.scipy.special.erf(act * (1.0 / math.sqrt(2.0))))
    density = jnp.exp(-0.5 * act * act) * (1.0 / math.sqrt(2.0 * math.pi))
    return (act * cdf, cdf + act * density)


class Place:
    def __init__(self):
        grp, wide = lax.axis_index("grp"), lax.axis_index("wide")
        self.grp, self.wide = grp, wide
        self.z_lo, self.core = grp // 2, grp % 2
        self.y, self.x, self.z_hi = wide // 8, wide // 2 % 4, wide % 2

    def x_next(self, step):
        return (self.grp, (self.y * 4 + self.x_at(step)) * 2 + self.z_hi)

    def y_next(self, step):
        return (self.grp, (self.y_at(step) * 4 + self.x) * 2 + self.z_hi)

    def x_at(self, step):
        return (self.x + step + 4) % 4

    def y_at(self, step):
        return (self.y + step + 4) % 4

    def mirror_z(self):
        return ((1 - self.z_lo) * 2 + self.core, (self.y * 4 + self.x) * 2 + 1 - self.z_hi)

    def next_z(self):
        return ((1 - self.z_lo) * 2 + self.core, self.wide)

    def sibling(self):
        return (self.z_lo * 2 + 1 - self.core, self.wide)


def enter(partners):
    barrier = pltpu.get_barrier_semaphore()
    for partner in partners:
        pl.semaphore_signal(barrier, inc=1, device_id=partner, device_id_type=MESH)
    pl.semaphore_wait(barrier, len(partners))


def part(entry):
    return pl.ds(entry[0], entry[1]) if isinstance(entry, tuple) else entry


def extent(entry):
    return entry[1] if isinstance(entry, tuple) else None


class Copies:
    def __init__(self, send_sem, recv_sem):
        self.numbers = itertools.count()
        self.send_sem, self.recv_sem = send_sem, recv_sem
        self.started = []

    def send(self, src, dst, device):
        i = next(self.numbers)
        copy = pltpu.make_async_remote_copy(
            src_ref=src,
            dst_ref=dst,
            send_sem=self.send_sem.at[i],
            recv_sem=self.recv_sem.at[i],
            device_id=device,
            device_id_type=MESH,
        )
        copy.start()
        self.started.append(copy)
        return copy

    def finish(self):
        for copy in self.started:
            copy.wait_send()


class Task:
    def __init__(self, link, cost, needs, run, rank=0):
        self.link, self.cost, self.run, self.rank = link, cost, run, rank
        self.needs = [need for need in needs if need is not None]
        self.copy, self.landed, self.done = None, False, None


def plan(tasks):
    free, now, order, left = {}, 0.0, [], list(tasks)
    while left:
        able = [
            (max([need.done for need in task.needs], default=0.0), task)
            for task in left
            if all(need.done is not None for need in task.needs)
        ]
        soon = [pair for pair in able if pair[0] <= now]
        if soon:
            ready, task = min(soon, key=lambda pair: (pair[1].link == "core", pair[1].rank, pair[0]))
        else:
            ready, task = min(able, key=lambda pair: (pair[0], pair[1].rank))
        now = max(now, ready)
        if task.link == "core":
            now += task.cost
            task.done = now
        else:
            now += 0.15
            rate = {"sibling": 0.4, "local": 0.4}.get(task.link, 0.0445)
            free[task.link] = max(now, free.get(task.link, 0.0)) + task.cost * 1e-6 / rate
            task.done = free[task.link] + 1.5
        order.append(task)
        left.remove(task)
    return order


def carry_out(order):
    for task in order:
        for need in task.needs:
            land(need)
        task.copy = task.run()
    for task in order:
        land(task)


def land(task):
    if task.copy is not None and not task.landed:
        if task.link == "local":
            task.copy.wait()
        else:
            task.copy.wait_recv()
        task.landed = True


def cut_y(region, half):
    return ((half * 2, 2), region[1], region[2])


def cut_x(region, half):
    return (region[0], (half * 2, 2), region[2])


def cut_z(region, half):
    return (region[0], region[1], half)


def chunks(region):
    return math.prod(extent(entry) or 1 for entry in region)


def gather_kernel(splits, *refs):
    count = len(splits)
    ins, refs = refs[:count], refs[count:]
    (dino_in, siglip_in, sam_in), refs = refs[:3], refs[3:]
    (first_out, second_out, dino_out, siglip_out, sam_out), refs = refs[:5], refs[5:]
    dino_all, mixed_all, pre, cells, local_sem, send_sem, recv_sem = refs
    outs = (dino_all, mixed_all, first_out, second_out)
    at = Place()
    enter(
        [
            at.x_next(1),
            at.x_next(-1),
            at.y_next(1),
            at.y_next(-1),
            at.mirror_z(),
            at.next_z(),
            at.sibling(),
        ]
    )
    copies = Copies(send_sem, recv_sem)
    tasks = []

    def lanes(k, s):
        start = at.core * sum(splits[k]) + sum(splits[k][:s])
        return pl.ds(pl.multiple_of(start * LANE, LANE), splits[k][s] * LANE)

    def view(k, s, region):
        return outs[k].at[part(region[0]), part(region[1]), part(region[2]), :, lanes(k, s)]

    def keep(k):
        def run():
            copy = pltpu.make_async_copy(
                ins[k], outs[k].at[at.y, at.x, at.z_hi], local_sem.at[k]
            )
            copy.start()
            return copy

        return Task("local", ins[k].shape[0] * ins[k].shape[1] * 2, [], run, k)

    kept = [keep(k) for k in range(count)]
    tasks.extend(kept)

    def send(k, s, region, link, device, needs):
        def run():
            src = ins[k].at[:, lanes(k, s)] if region is own else view(k, s, region)
            return copies.send(src, view(k, s, region), device)

        size = chunks(region) * ins[k].shape[0] * splits[k][s] * LANE * 2
        task = Task(link, size, needs, run, k)
        tasks.append(task)
        return task

    own = (at.y, at.x, at.z_hi)
    found = [[] for _ in range(count)]

    def arrive(k, s, region, task):
        half = send(k, s, region, "sibling", at.sibling(), [task])
        found[k] += [task, half]
        return task

    def across(k, s, needs):
        task = send(k, s, own, "mirror", at.mirror_z(), needs)
        return [arrive(k, s, (at.y, at.x, 1 - at.z_hi), task)]

    def across_both(k, s, needs):
        first = send(k, s, ((2 - 2 * at.z_lo, 2), ALL, at.z_hi), "mirror", at.mirror_z(), needs)
        here = ((2 * at.z_lo, 2), ALL, 1 - at.z_hi)
        arrive(k, s, here, first)
        second = send(k, s, here, "next", at.next_z(), [first])
        arrive(k, s, ((2 - 2 * at.z_lo, 2), ALL, 1 - at.z_hi), second)

    def around(k, s, axis, block, cut, needs):
        place, device = (at.x_at, at.x_next) if axis == "x" else (at.y_at, at.y_next)
        here = own if cut is None else block(place(0))
        back, ahead, over = block(place(-1)), block(place(1)), block(place(2))
        up = arrive(k, s, back, send(k, s, here, axis + "+", device(1), needs))
        down = arrive(k, s, ahead, send(k, s, here, axis + "-", device(-1), needs))
        got = [up, down]
        if cut is not None:
            task = send(k, s, cut(back, 0), axis + "+", device(1), [up])
            got.append(arrive(k, s, cut(over, 0), task))
            task = send(k, s, cut(ahead, 1), axis + "-", device(-1), [down])
            got.append(arrive(k, s, cut(over, 1), task))
        elif k % 2 == 0:
            task = send(k, s, back, axis + "+", device(1), [up])
            got.append(arrive(k, s, over, task))
        else:
            task = send(k, s, ahead, axis + "-", device(-1), [down])
            got.append(arrive(k, s, over, task))
        return got

    for k in range(count):
        mine = [kept[k]]
        got = across(k, 0, [])
        got = mine + got + around(k, 0, "y", lambda c: (c, at.x, BOTH), cut_z, mine + got)
        around(k, 0, "x", lambda c: (ALL, c, BOTH), cut_y, got)
        got = across(k, 1, [])
        got = mine + got + around(k, 1, "x", lambda c: (at.y, c, BOTH), cut_z, mine + got)
        around(k, 1, "y", lambda c: (c, ALL, BOTH), cut_x, got)
        got = mine + around(k, 2, "x", lambda c: (at.y, c, at.z_hi), None, [])
        got = got + around(k, 2, "y", lambda c: (c, ALL, at.z_hi), cut_x, got)
        across_both(k, 2, got)
        got = mine + around(k, 3, "y", lambda c: (c, at.x, at.z_hi), None, [])
        got = got + around(k, 3, "x", lambda c: (ALL, c, at.z_hi), cut_y, got)
        across_both(k, 3, got)

    def mix(rows_ref, begin, weights, lane, width, count, mask, write):
        rows = rows_ref[begin : begin + 256, :]
        step = weights.shape[3] * 16
        for half in range(2):
            block = weights[2 * half : 2 * half + 2, :, :, :, lane : lane + rows.shape[1]]
            mixed = lax.dot_general(
                rows,
                block.reshape(step, rows.shape[1]),
                (((1,), (1,)), ((), ())),
                preferred_element_type=jnp.float32,
            )
            side = rows[:, half * step : (half + 1) * step].astype(jnp.float32)
            pre[:, half * step : (half + 1) * step] = side + mixed

        @pl.loop(0, 8)
        def _(i):
            spot = pl.ds(pl.multiple_of(i * 32, 32), 32)
            values = pre[spot, :width]
            write(spot, layer_norm(values, count, mask).astype(jnp.bfloat16))

    def dino():
        def write(spot, values):
            dino_out[spot, :] = values

        mix(dino_in, 0, dino_all, 0, 1536, 1536, None, write)

    def siglip():
        def write(spot, values):
            siglip_out[spot, :] = values

        column = lax.broadcasted_iota(jnp.int32, (1, 1280), 1)
        mask = (column % 40 < 36).astype(jnp.float32)
        mix(siglip_in, 0, mixed_all, 1280, 1280, 1152, mask, write)

    def sam(b):
        def run():
            def write(spot, values):
                cells[spot, :] = values

            mix(sam_in, b * 256, mixed_all, 0, 1280, 1280, None, write)
            block = lax.broadcasted_iota(jnp.int32, (64, 256), 0)
            cell = lax.broadcasted_iota(jnp.int32, (64, 256), 1)
            member = ((cell >= 4 * block) & (cell < 4 * block + 4)).astype(jnp.bfloat16)
            total = jnp.dot(member, cells[...], preferred_element_type=jnp.float32)
            sam_out[b * 64 : b * 64 + 64, :] = (total * 0.25).astype(jnp.bfloat16)

        return run

    tasks.append(Task("core", 4.0, found[0] + [kept[0]], dino))
    tasks.append(Task("core", 4.0, found[1] + [kept[1]], siglip))
    for b in range(4):
        tasks.append(Task("core", 3.5, found[1] + [kept[1]], sam(b)))
    carry_out(plan(tasks))
    copies.finish()


def gather_and_map(shards, rows, splits):
    whole = pl.BlockSpec(memory_space=pl.ANY)
    inside = pl.BlockSpec(memory_space=pltpu.VMEM)
    shapes = [(4, 4, 2) + shard.shape for shard in shards]
    semaphores = pltpu.SemaphoreType.DMA((72 * len(shards),))
    first, second, dino, siglip, sam = pl.pallas_call(
        functools.partial(gather_kernel, splits),
        out_shape=[
            jax.ShapeDtypeStruct(shapes[2], jnp.bfloat16),
            jax.ShapeDtypeStruct(shapes[3], jnp.bfloat16),
            jax.ShapeDtypeStruct((256, 1536), jnp.bfloat16),
            jax.ShapeDtypeStruct((256, 1280), jnp.bfloat16),
            jax.ShapeDtypeStruct((256, 1280), jnp.bfloat16),
        ],
        in_specs=[whole] * len(shards) + [inside] * 3,
        out_specs=[whole] * 2 + [inside] * 3,
        scratch_shapes=[
            pltpu.VMEM(shapes[0], jnp.bfloat16),
            pltpu.VMEM(shapes[1], jnp.bfloat16),
            pltpu.VMEM((256, 1536), jnp.float32),
            pltpu.VMEM((256, 1280), jnp.bfloat16),
            pltpu.SemaphoreType.DMA((len(shards),)),
            semaphores,
            semaphores,
        ],
        compiler_params=pltpu.CompilerParams(
            collective_id=0, has_side_effects=True, vmem_limit_bytes=60 * 1024 * 1024
        ),
        name="gather_and_map",
    )(*shards, *rows)
    return [first.reshape(1280, -1), second.reshape(768, -1), dino, siglip, sam]


WIDTHS = (1536, 1280, 1280)
FIRST_SPLITS = ((1, 0, 1, 1), (0, 1, 1, 1), (1, 0, 1, 1))
SECOND_SPLITS = ((0, 2, 2, 2), (2, 0, 1, 2), (0, 2, 2, 1))


def adaptor_kernel(factor, *refs):
    (rows_in, *targets), refs = refs[:4], refs[4:]
    (first_in, second_in), refs = refs[:2], refs[2:]
    outs, refs = refs[:6], refs[6:]
    (first_all, second_all, act, pred, slope), refs = refs[:5], refs[5:]
    kinds = []
    for _ in range(8):
        kinds.append(refs[:3])
        refs = refs[3:]
    normed, normed_too, hidden, hidden_too, grad_act, grad_act_too, grad_pred, grad_pred_too = kinds
    sums, last, refs = refs[:6], refs[6:12], refs[12:]
    spare, (local_sem, send_sem, recv_sem) = iter(refs[:-3]), refs[-3:]
    splits = FIRST_SPLITS + SECOND_SPLITS
    at = Place()
    enter(
        [
            at.x_next(1),
            at.x_next(-1),
            at.y_next(1),
            at.y_next(-1),
            at.mirror_z(),
            at.next_z(),
            at.sibling(),
        ]
    )
    copies = Copies(send_sem, recv_sem)
    tasks = []

    def add_task(*args):
        tasks.append(Task(*args))
        return tasks[-1]

    begins = (0, 1536, 2816)

    def fetch(i, src, dst, begin, width, rank):
        def run():
            columns = pl.ds(begin, width)
            copy = pltpu.make_async_copy(src.at[:, columns], dst.at[:, columns], local_sem.at[i])
            copy.start()
            return copy

        return add_task("local", src.shape[0] * width, [], run, rank)

    fetched = []
    for t in range(3):
        fetched.append(
            [
                fetch(2 * t, first_in, first_all, 768 * t, 768, -1),
                fetch(2 * t + 1, second_in, second_all, begins[t], WIDTHS[t], -1),
            ]
        )

    def pick(t):
        spot = lax.broadcasted_iota(jnp.int32, (256, 512), 0)
        source = lax.broadcasted_iota(jnp.int32, (256, 512), 1)
        straight = spot // 8 * 16 + spot % 8
        flags = jnp.dot(
            (source == straight).astype(jnp.bfloat16),
            rows_in[:, 1280:],
            preferred_element_type=jnp.float32,
        )
        shift = jnp.where(flags[:, t : t + 1] > 0.5, 0, 8)
        normed[t][...] = jnp.dot(
            (source == straight + shift).astype(jnp.bfloat16),
            rows_in[:, :1280],
            preferred_element_type=jnp.float32,
        ).astype(jnp.bfloat16)

    def forward(t):
        def run():
            pick(t)
            act[...] = jnp.dot(
                normed[t][...],
                first_all[:, 768 * t : 768 * t + 768],
                preferred_element_type=jnp.float32,
            )

            @pl.loop(0, 16)
            def _(i):
                spot = pl.ds(pl.multiple_of(i * 16, 16), 16)
                hid, tilt = gelu_pair(act[spot, :])
                hidden[t][spot, :] = hid.astype(jnp.bfloat16)
                slope[spot, :] = tilt

        return run

    def backward(t):
        width = WIDTHS[t]

        def run():
            second = second_all[:, begins[t] : begins[t] + width]
            pred[:, :width] = jnp.dot(
                hidden[t][...], second, preferred_element_type=jnp.float32
            )

            @pl.loop(0, 16)
            def _(i):
                spot = pl.ds(pl.multiple_of(i * 16, 16), 16)
                wanted = targets[t][spot, :].astype(jnp.float32)
                grad = factor * (pred[spot, :width] - wanted)
                grad_pred[t][spot, :] = grad.astype(jnp.bfloat16)

            act[...] = lax.dot_general(
                grad_pred[t][...],
                second,
                (((1,), (1,)), ((), ())),
                preferred_element_type=jnp.float32,
            )

            @pl.loop(0, 16)
            def _(i):
                spot = pl.ds(pl.multiple_of(i * 16, 16), 16)
                grad_act[t][spot, :] = (act[spot, :] * slope[spot, :]).astype(jnp.bfloat16)

        return run

    def half(width, core):
        return pl.ds(pl.multiple_of(core * (width // 2), LANE), width // 2)

    def outer(left, right):
        return lax.dot_general(
            left, right, (((0,), (0,)), ((), ())), preferred_element_type=jnp.float32
        )

    def first_grads(t):
        def run():
            mine, other = grad_act[t][:, half(768, at.core)], grad_act_too[t][...]
            for part_of in range(2):
                columns = slice(640 * part_of, 640 * part_of + 640)
                total = outer(normed[t][:, columns], mine)
                total = total + outer(normed_too[t][:, columns], other)
                sums[t][2 * part_of : 2 * part_of + 2] = total.reshape(2, 4, 2, 40, 384)

        return run

    def second_grads(t):
        width = WIDTHS[t]

        def run():
            mine, other = grad_pred[t][:, half(width, at.core)], grad_pred_too[t][...]
            for part_of in range(2):
                columns = slice(384 * part_of, 384 * part_of + 384)
                total = outer(hidden[t][:, columns], mine)
                total = total + outer(hidden_too[t][:, columns], other)
                sums[3 + t][2 * part_of : 2 * part_of + 2] = total.reshape(
                    2, 4, 2, 24, width // 2
                )

        return run

    def share(src, dst, width, needs, rank):
        def run():
            whole = src if width is None else src.at[:, half(width, 1 - at.core)]
            return copies.send(whole, dst, at.sibling())

        return add_task("sibling", 256 * dst.shape[1] * 2, needs, run, rank)

    ready, before = {}, None
    for t in range(3):
        one = add_task("core", 4.0, [fetched[t][0], before], forward(t), 10 * t + 2)
        got_normed = share(normed[t], normed_too[t], None, [one], t)
        got_hidden = share(hidden[t], hidden_too[t], None, [one], t)
        before = add_task("core", 4.0, [fetched[t][1], one], backward(t), 10 * t + 2)
        got_act = share(grad_act[t], grad_act_too[t], 768, [before], t)
        got_pred = share(grad_pred[t], grad_pred_too[t], WIDTHS[t], [before], t)
        ready[t] = add_task("core", 1.5, [before, got_normed, got_act], first_grads(t), 10 * t + 1)
        ready[3 + t] = add_task(
            "core", 1.5, [before, got_hidden, got_pred], second_grads(t), 10 * t + 1
        )

    def lanes(k, s):
        return pl.ds(sum(splits[k][:s]) * LANE, splits[k][s] * LANE)

    def view(k, s, region):
        return sums[k].at[part(region[0]), part(region[1]), part(region[2]), :, lanes(k, s)]

    def send(k, s, region, link, device, needs):
        room = next(spare)

        def run():
            return copies.send(view(k, s, region), room, device)

        size = chunks(region) * sums[k].shape[3] * splits[k][s] * LANE * 4
        task = add_task(link, size, needs, run, k % 3)
        task.room = room
        return task

    def add(k, s, region, sent, needs):
        sizes = [extent(entry) for entry in region]
        steps = [size or 1 for size in sizes]
        count = steps[0] * steps[1] * steps[2]

        def run():
            @pl.loop(0, count)
            def _(i):
                spots = (i // (steps[1] * steps[2]), i // steps[2] % steps[1], i % steps[2])
                there = tuple(spot for spot, size in zip(spots, sizes) if size)
                here = tuple(
                    spot + entry[0] if size else entry
                    for spot, size, entry in zip(spots, sizes, region)
                )
                where = here + (slice(None), lanes(k, s))
                total = sums[k][where]
                for task in sent:
                    total = total + task.room[there + (slice(None), slice(None))]
                sums[k][where] = total

        size = count * sums[k].shape[3] * splits[k][s] * LANE * 4
        return add_task("core", 0.1 + size * 0.5e-6, sent + needs, run, -1)

    def across(k, s, needs):
        sent = send(k, s, (at.y, at.x, 1 - at.z_hi), "mirror", at.mirror_z(), needs)
        return [add(k, s, (at.y, at.x, at.z_hi), [sent], needs)]

    def across_both(k, s, needs):
        mine, other = (2 * at.z_lo, 2), (2 - 2 * at.z_lo, 2)
        sent = send(k, s, (other, ALL, 1 - at.z_hi), "next", at.next_z(), needs)
        added = add(k, s, (mine, ALL, 1 - at.z_hi), [sent], needs)
        sent = send(k, s, (mine, ALL, 1 - at.z_hi), "mirror", at.mirror_z(), [added])
        return [add(k, s, (other, ALL, at.z_hi), [sent], needs)]

    def around(k, s, axis, block, cut, needs):
        place, device = (at.x_at, at.x_next) if axis == "x" else (at.y_at, at.y_next)
        here, over, back, ahead = (block(place(step)) for step in (0, 2, -1, 1))
        up, down = [], []
        if cut is not None:
            sent = send(k, s, cut(over, 0), axis + "+", device(1), needs)
            up.append(add(k, s, cut(ahead, 0), [sent], needs))
            sent = send(k, s, cut(over, 1), axis + "-", device(-1), needs)
            down.append(add(k, s, cut(back, 1), [sent], needs))
        elif k % 2 == 0:
            sent = send(k, s, over, axis + "+", device(1), needs)
            up.append(add(k, s, ahead, [sent], needs))
        else:
            sent = send(k, s, over, axis + "-", device(-1), needs)
            down.append(add(k, s, back, [sent], needs))
        one = send(k, s, ahead, axis + "+", device(1), needs + up)
        two = send(k, s, back, axis + "-", device(-1), needs + down)
        return [add(k, s, here, [one, two], needs)]

    def settle(k, s, needs):
        own = (at.y, at.x, at.z_hi)
        where = (slice(None), lanes(k, s))

        def swap():
            return copies.send(view(k, s, own), last[k].at[:, lanes(k, s)], at.next_z())

        def total():
            value = sums[k][own + where] + last[k][where]
            outs[k][(at.core,) + where] = value

        def share_total():
            place = outs[k].at[at.core, :, lanes(k, s)]
            return copies.send(place, place, at.sibling())

        size = sums[k].shape[3] * splits[k][s] * LANE * 4
        swapped = add_task("next", size, needs, swap, -1)
        added = add_task("core", 0.2, needs + [swapped], total, -1)
        add_task("sibling", size, [added], share_total, -1)

    for k in range(6):
        done = [ready[k]]
        for s in range(4):
            if splits[k][s] == 0:
                continue
            if s == 0:
                got = around(k, s, "x", lambda c: (ALL, c, BOTH), cut_y, done)
                got = around(k, s, "y", lambda c: (c, at.x, BOTH), cut_z, got)
                got = across(k, s, got)
            elif s == 1:
                got = around(k, s, "y", lambda c: (c, ALL, BOTH), cut_x, done)
                got = around(k, s, "x", lambda c: (at.y, c, BOTH), cut_z, got)
                got = across(k, s, got)
            elif s == 2:
                got = across_both(k, s, done)
                got = around(k, s, "y", lambda c: (c, ALL, at.z_hi), cut_x, got)
                got = around(k, s, "x", lambda c: (at.y, c, at.z_hi), None, got)
            else:
                got = across_both(k, s, done)
                got = around(k, s, "x", lambda c: (ALL, c, at.z_hi), cut_y, got)
                got = around(k, s, "y", lambda c: (c, at.x, at.z_hi), None, got)
            settle(k, s, got)
    carry_out(plan(tasks))
    copies.finish()


def adaptor_gradients(rows, targets, first_all, second_all, factor):
    inside = pl.BlockSpec(memory_space=pltpu.VMEM)
    whole = pl.BlockSpec(memory_space=pl.ANY)
    splits = FIRST_SPLITS + SECOND_SPLITS
    depth = [40] * 3 + [24] * 3
    width = [384] * 3 + [w // 2 for w in WIDTHS]

    def rooms():
        plane, line = [(2, 2), (2, 2), (4, 2), (4, 2)], [(), (), (2,), (2,)]
        column, spot = [(2,), (2,), (4,), (4,)], [(), (), ()]
        leads = [plane + line + [()]] * 2 + [[(2, 4), (2, 4)] + column + spot] * 2
        for k in range(6):
            for s in range(4):
                if splits[k][s]:
                    for lead in leads[s]:
                        yield pltpu.VMEM(lead + (depth[k], splits[k][s] * LANE), jnp.float32)

    def three(*widths):
        return [pltpu.VMEM((256, w), jnp.bfloat16) for w in widths]

    halves = [w // 2 for w in WIDTHS]
    semaphores = pltpu.SemaphoreType.DMA((230,))
    return pl.pallas_call(
        functools.partial(adaptor_kernel, factor),
        out_shape=[
            jax.ShapeDtypeStruct((2, d, w), jnp.float32) for d, w in zip(depth, width)
        ],
        in_specs=[inside] * 4 + [whole] * 2,
        out_specs=[inside] * 6,
        scratch_shapes=[
            pltpu.VMEM(first_all.shape, jnp.bfloat16),
            pltpu.VMEM(second_all.shape, jnp.bfloat16),
            pltpu.VMEM((256, 768), jnp.float32),
            pltpu.VMEM((256, 1536), jnp.float32),
            pltpu.VMEM((256, 768), jnp.float32),
            *three(*[1280] * 6),
            *three(*[768] * 6),
            *three(*[768] * 3),
            *three(*[384] * 3),
            *three(*WIDTHS),
            *three(*halves),
            *[pltpu.VMEM((4, 4, 2, d, w), jnp.float32) for d, w in zip(depth, width)],
            *[pltpu.VMEM((d, w), jnp.float32) for d, w in zip(depth, width)],
            *rooms(),
            pltpu.SemaphoreType.DMA((6,)),
            semaphores,
            semaphores,
        ],
        compiler_params=pltpu.CompilerParams(
            collective_id=1, has_side_effects=True, vmem_limit_bytes=62 * 1024 * 1024
        ),
        name="adaptor_gradients",
    )(rows, *targets, first_all, second_all)


def spread(width, group, room):
    rows = lax.broadcasted_iota(jnp.int32, (width, width // group * room), 0)
    columns = lax.broadcasted_iota(jnp.int32, (width, width // group * room), 1)
    return (rows // group * room + rows % group == columns).astype(jnp.bfloat16)


def place_columns(values, table):
    return jnp.dot(values, table, preferred_element_type=jnp.float32).astype(jnp.bfloat16)


def student_rows(student_feats, indices):
    normed = layer_norm(student_feats[0].astype(jnp.float32)).astype(jnp.bfloat16)
    patches = jnp.arange(256, dtype=jnp.int32)
    flags = jnp.stack([index[0] == patches for index in indices], axis=-1).astype(jnp.bfloat16)
    rows = jnp.concatenate([normed, jnp.pad(flags, ((0, 0), (0, LANE - 3)))], axis=-1)
    grid = rows.reshape(16, 16, -1)
    return jnp.concatenate(
        [grid.reshape(32, 8, -1), grid[:, ::-1].reshape(32, 8, -1)], axis=1
    )


def body(
    student_feats,
    dino_in,
    siglip_in,
    sam_in,
    dino_proj,
    siglip_proj,
    sam_proj,
    dino_index,
    siglip_index,
    sam_index,
    dino_first,
    dino_second,
    siglip_first,
    siglip_second,
    sam_first,
    sam_second,
):
    images_total = student_feats.shape[0] * 128
    rows = lax.all_to_all(
        student_rows(student_feats, (dino_index, siglip_index, sam_index)),
        "wide",
        split_axis=0,
        concat_axis=0,
        tiled=True,
    )
    siglip_room = spread(1152, 36, 40)
    hidden_room = spread(640, 20, 24)
    siglip_turned = jnp.pad(place_columns(siglip_proj.T, siglip_room), ((0, 4), (0, 0)))
    firsts = place_columns(
        jnp.concatenate([dino_first, siglip_first, sam_first], axis=0), hidden_room
    ).reshape(3, 40, 768)
    seconds = jnp.concatenate(
        [dino_second, place_columns(siglip_second, siglip_room), sam_second], axis=1
    )
    first_all, second_all, *targets = gather_and_map(
        [
            dino_proj.T,
            jnp.concatenate([sam_proj.T, siglip_turned], axis=1),
            jnp.concatenate([*firsts], axis=1),
            jnp.pad(seconds, ((0, 4), (0, 0))),
        ],
        [
            dino_in.reshape(256, -1),
            place_columns(siglip_in.reshape(256, -1), siglip_room),
            sam_in.reshape(1024, -1),
        ],
        ((1, 1, 2, 2), (2, 2, 3, 3), (2, 2, 3, 2), (3, 3, 5, 5)),
    )
    sums = adaptor_gradients(
        rows.reshape(512, -1), targets, first_all, second_all, 2.0 / images_total
    )
    joined = [jnp.concatenate([total[0], total[1]], axis=-1) for total in sums]
    firsts = [total.reshape(40, 32, 24)[..., :20].reshape(40, 640) for total in joined[:3]]
    seconds = [total[:20] for total in joined[3:]]
    siglip_two = seconds[1].reshape(20, 32, 40)[..., :36].reshape(20, 1152)
    return (firsts[0], seconds[0], firsts[1], siglip_two, firsts[2], seconds[2])


def solution(mesh):
    shared = P("wide", None)
    return jax.shard_map(
        body,
        mesh=mesh,
        in_specs=(
            P(("grp", "wide"), None, None),
            *[P("grp", "wide", None)] * 3,
            *[P(None, "wide")] * 3,
            *[P(("grp", "wide"), None)] * 3,
            *[shared] * 6,
        ),
        out_specs=(shared,) * 6,
        check_vma=False,
    )
```

```python
import functools
import itertools
import math

import jax
import jax.numpy as jnp
from jax import lax
from jax.experimental import pallas as pl
from jax.experimental.pallas import tpu as pltpu
from jax.sharding import PartitionSpec as P

MESH = pl.DeviceIdType.MESH
LANE = 128
ALL = (0, 4)
BOTH = (0, 2)


def layer_norm(values, count=None, mask=None):
    count = values.shape[-1] if count is None else count
    centered = values - jnp.sum(values, axis=-1, keepdims=True) * (1.0 / count)
    if mask is not None:
        centered = centered * mask
    variance = jnp.sum(centered * centered, axis=-1, keepdims=True) * (1.0 / count)
    return centered * lax.rsqrt(variance + 1e-05)


def gelu_pair(act):
    cdf = 0.5 * (1.0 + jax.scipy.special.erf(act * (1.0 / math.sqrt(2.0))))
    density = jnp.exp(-0.5 * act * act) * (1.0 / math.sqrt(2.0 * math.pi))
    return (act * cdf, cdf + act * density)


class Place:
    def __init__(self):
        grp, wide = lax.axis_index("grp"), lax.axis_index("wide")
        self.grp, self.wide = grp, wide
        self.z_lo, self.core = grp // 2, grp % 2
        self.y, self.x, self.z_hi = wide // 8, wide // 2 % 4, wide % 2

    def x_next(self, step):
        return (self.grp, (self.y * 4 + self.x_at(step)) * 2 + self.z_hi)

    def y_next(self, step):
        return (self.grp, (self.y_at(step) * 4 + self.x) * 2 + self.z_hi)

    def x_at(self, step):
        return (self.x + step + 4) % 4

    def y_at(self, step):
        return (self.y + step + 4) % 4

    def mirror_z(self):
        return ((1 - self.z_lo) * 2 + self.core, (self.y * 4 + self.x) * 2 + 1 - self.z_hi)

    def next_z(self):
        return ((1 - self.z_lo) * 2 + self.core, self.wide)

    def sibling(self):
        return (self.z_lo * 2 + 1 - self.core, self.wide)


def enter(partners):
    barrier = pltpu.get_barrier_semaphore()
    for partner in partners:
        pl.semaphore_signal(barrier, inc=1, device_id=partner, device_id_type=MESH)
    pl.semaphore_wait(barrier, len(partners))


def part(entry):
    return pl.ds(entry[0], entry[1]) if isinstance(entry, tuple) else entry


def extent(entry):
    return entry[1] if isinstance(entry, tuple) else None


class Copies:
    def __init__(self, send_sem, recv_sem):
        self.send_sem, self.recv_sem = send_sem, recv_sem
        self.started = []

    def send(self, src, dst, device):
        i = len(self.started)
        if i >= SENDS:
            self.started[i - SENDS].wait_send()
        copy = pltpu.make_async_remote_copy(
            src_ref=src,
            dst_ref=dst,
            send_sem=self.send_sem.at[i % SENDS],
            recv_sem=self.recv_sem.at[i],
            device_id=device,
            device_id_type=MESH,
        )
        copy.start()
        self.started.append(copy)
        return copy

    def finish(self):
        for copy in self.started[-SENDS:]:
            copy.wait_send()


class Task:
    def __init__(self, link, cost, needs, run, rank=0):
        self.link, self.cost, self.run, self.rank = link, cost, run, rank
        self.needs = [need for need in needs if need is not None]
        self.copy, self.landed, self.done = None, False, None


BACKLOG = 2.0
LATENCY = 4.0
RATES = {"sibling": 0.4, "local": 0.65}


def span(task):
    return task.cost if task.link == "core" else task.cost * 1e-6 / RATES.get(task.link, 0.0445)


def plan(tasks):
    tails = {id(task): 0.0 for task in tasks}
    for task in reversed(tasks):
        tail = tails[id(task)] + span(task) + (0.0 if task.link == "core" else 1.5)
        for need in task.needs:
            tails[id(need)] = max(tails[id(need)], tail)
    free, now, order, left = {}, 0.0, [], list(tasks)
    while left:
        best = None
        for task in left:
            ready = 0.0
            for need in task.needs:
                if need.done is None:
                    break
                ready = max(ready, need.done)
            else:
                if task.link != "core":
                    ready = max(ready, free.get(task.link, 0.0) - BACKLOG)
                key = (max(ready, now), task.link == "core", task.rank, -tails[id(task)])
                if best is None or key < best[0]:
                    best = (key, task)
        (now, *_), task = best
        if task.link == "core":
            now += task.cost
            task.done = now
        else:
            now += 0.05
            free[task.link] = max(now, free.get(task.link, 0.0)) + span(task)
            task.done = free[task.link] + LATENCY
        order.append(task)
        left.remove(task)
    return order


def carry_out(order):
    for task in order:
        for need in task.needs:
            land(need)
        task.copy = task.run()
    for task in order:
        land(task)


def land(task):
    if task.copy is not None and not task.landed:
        if task.link == "local":
            task.copy.wait()
        else:
            task.copy.wait_recv()
        task.landed = True


WIDTHS = (1536, 1280, 1280)
STUDENT = 1280 + LANE
PROJ_SPLITS = ((2, 1, 2, 1), (1, 2, 1, 1), (1, 1, 1, 2))
FIRST_SPLITS = ((1, 1, 1, 0), (1, 1, 0, 1), (1, 0, 1, 1))
SECOND_SPLITS = ((1, 2, 1, 2), (1, 1, 2, 1), (1, 2, 1, 1))
GRAD_SPLITS = (
    ((1, 0, 1, 1), (0, 1, 1, 1), (1, 1, 1, 0)),
    ((1, 1, 2, 2), (1, 1, 1, 2), (1, 1, 2, 1)),
)
COPIES = 642
SENDS = 48
ORDER = (2, 0, 1)
LOCALS = 24


def cut_y(region, half):
    return ((half * 2, 2), region[1], region[2])


def cut_x(region, half):
    return (region[0], (half * 2, 2), region[2])


def cut_z(region, half):
    return (region[0], region[1], half)


def chunks(region):
    return math.prod(extent(entry) or 1 for entry in region)


class Refs:
    def __init__(self, refs):
        self.refs = list(refs)

    def take(self, count):
        taken, self.refs = self.refs[:count], self.refs[count:]
        return taken


def kernel(factor, *refs):
    refs = Refs(refs)
    shards, inputs, (student_in,) = refs.take(9), refs.take(3), refs.take(1)
    outs, weights = refs.take(6), refs.take(6)
    hop_y, ((rows_y,), hop_x, (rows_all,), hop_z) = refs.take(2), (
        refs.take(1),
        refs.take(2),
        refs.take(1),
        refs.take(2),
    )
    projs, (first_all, second_all, rows_in) = refs.take(3), refs.take(3)
    whole = projs + weights
    held, targets = refs.take(3), refs.take(3)
    (cells, act, pred, slope) = refs.take(4)
    normed, normed_too, hidden, hidden_too = (refs.take(3) for _ in range(4))
    grad_act, grad_act_too, grad_pred, grad_pred_too = (refs.take(3) for _ in range(4))
    sums, last = refs.take(6), refs.take(6)
    spare, (local_sem, send_sem, recv_sem) = iter(refs.refs[:-3]), refs.refs[-3:]
    at = Place()
    enter(
        [
            at.x_next(1),
            at.x_next(-1),
            at.y_next(1),
            at.y_next(-1),
            at.mirror_z(),
            at.next_z(),
            at.sibling(),
        ]
    )
    copies = Copies(send_sem, recv_sem)
    locals_used = itertools.count()
    tasks = []
    own = (at.y, at.x, at.z_hi)

    def add_task(*args):
        tasks.append(Task(*args))
        return tasks[-1]

    def size_of(ref):
        return math.prod(ref.shape) * 2

    def move(src, dst, needs, rank):
        def run():
            copy = pltpu.make_async_copy(src, dst, local_sem.at[next(locals_used)])
            copy.start()
            return copy

        return add_task("local", size_of(dst), needs, run, rank)

    def carry(src, dst, link, device, needs, rank):
        def run():
            return copies.send(src, dst, device)

        return add_task(link, size_of(dst), needs, run, rank)

    def spread_student():
        x_low, x_high = pl.ds(0, 2), pl.ds(2, 2)
        here = move(student_in.at[at.y], rows_y.at[at.y], [], 2)
        got = [here]
        got.append(
            carry(student_in.at[at.y_at(1)], rows_y.at[at.y], "y+", at.y_next(1), [], 2)
        )
        got.append(
            carry(student_in.at[at.y_at(-1)], rows_y.at[at.y], "y-", at.y_next(-1), [], 2)
        )
        far = student_in.at[at.y_at(2)]
        up = carry(far.at[x_low], hop_y[0], "y+", at.y_next(1), [], 2)
        down = carry(far.at[x_high], hop_y[1], "y-", at.y_next(-1), [], 2)
        got.append(
            carry(hop_y[0], rows_y.at[at.y_at(-1), x_low], "y+", at.y_next(1), [up], 2)
        )
        got.append(
            carry(hop_y[1], rows_y.at[at.y_at(1), x_high], "y-", at.y_next(-1), [down], 2)
        )

        every, low, high = pl.ds(0, 4), pl.ds(0, 2), pl.ds(2, 2)
        mine = rows_all.at[every, at.x, at.z_hi]
        done = [move(rows_y.at[every, at.x], mine, got, 2)]
        for step, link in ((1, "x+"), (-1, "x-")):
            src = rows_y.at[every, at.x_at(step)]
            done.append(carry(src, mine, link, at.x_next(step), got, 2))
        far = at.x_at(2)
        up = carry(rows_y.at[low, far], hop_x[0], "x+", at.x_next(1), got, 2)
        down = carry(rows_y.at[high, far], hop_x[1], "x-", at.x_next(-1), got, 2)
        dst = rows_all.at[low, at.x_at(-1), at.z_hi]
        done.append(carry(hop_x[0], dst, "x+", at.x_next(1), [up], 2))
        dst = rows_all.at[high, at.x_at(1), at.z_hi]
        done.append(carry(hop_x[1], dst, "x-", at.x_next(-1), [down], 2))

        src = rows_all.at[low, every, at.z_hi]
        one = carry(src, hop_z[0], "mirror", at.mirror_z(), done, 2)
        src = rows_all.at[high, every, at.z_hi]
        two = carry(src, hop_z[1], "next", at.next_z(), done, 2)
        dst = rows_all.at[low, every, 1 - at.z_hi]
        one = carry(hop_z[0], dst, "next", at.next_z(), [one], 2)
        dst = rows_all.at[high, every, at.z_hi]
        two = carry(hop_z[1], dst, "mirror", at.mirror_z(), [two], 2)
        return move(rows_all, rows_in, done + [one, two], 2)

    def gather(k, splits, rank):
        shard, array = shards[k], whole[k]
        found = []

        def lanes(s):
            start = at.core * sum(splits) + sum(splits[:s])
            return pl.ds(pl.multiple_of(start * LANE, LANE), splits[s] * LANE)

        def view(s, region):
            return array.at[part(region[0]), part(region[1]), part(region[2]), :, lanes(s)]

        def send(s, region, link, device, needs):
            src = shard.at[:, lanes(s)] if region is own else view(s, region)
            return carry(src, view(s, region), link, device, needs, rank)

        def share(s, region, needs):
            found.append(send(s, region, "sibling", at.sibling(), needs))

        def across(s):
            return [kept, send(s, own, "mirror", at.mirror_z(), [])]

        def across_both(s, needs):
            mine, other = (2 * at.z_lo, 2), (2 - 2 * at.z_lo, 2)
            share(s, (ALL, ALL, at.z_hi), needs)
            one = send(s, (other, ALL, at.z_hi), "mirror", at.mirror_z(), needs)
            two = send(s, (mine, ALL, 1 - at.z_hi), "next", at.next_z(), [one])
            share(s, (mine, ALL, 1 - at.z_hi), [one])
            share(s, (other, ALL, 1 - at.z_hi), [two])
            found.extend(needs + [one, two])

        def last_around(s, axis, block, cut, needs):
            place = at.x_at if axis == "x" else at.y_at
            share(s, block(place(0)), needs)
            up, down, one, two = around(s, axis, block, cut, needs)[len(needs) :]
            share(s, block(place(-1)), [up])
            share(s, block(place(1)), [down])
            share(s, block(place(2)), [one, two])
            found.extend(needs + [up, down, one, two])

        def around(s, axis, block, cut, needs):
            place, device = (at.x_at, at.x_next) if axis == "x" else (at.y_at, at.y_next)
            here = own if cut is None else block(place(0))
            back, ahead = block(place(-1)), block(place(1))
            up = send(s, here, axis + "+", device(1), needs)
            down = send(s, here, axis + "-", device(-1), needs)
            got = needs + [up, down]
            if cut is not None:
                got.append(send(s, cut(back, 0), axis + "+", device(1), [up]))
                got.append(send(s, cut(ahead, 1), axis + "-", device(-1), [down]))
            elif k % 2 == 0:
                got.append(send(s, back, axis + "+", device(1), [up]))
            else:
                got.append(send(s, ahead, axis + "-", device(-1), [down]))
            return got

        def keep():
            start = pl.multiple_of(at.core * sum(splits) * LANE, LANE)
            columns = pl.ds(start, sum(splits) * LANE)
            return move(shard.at[:, columns], array.at[own + (slice(None), columns)], [], -1)

        kept = keep()
        found.append(kept)
        if splits[0]:
            got = around(0, "y", lambda c: (c, at.x, BOTH), cut_z, across(0))
            last_around(0, "x", lambda c: (ALL, c, BOTH), cut_y, got)
        if splits[1]:
            got = around(1, "x", lambda c: (at.y, c, BOTH), cut_z, across(1))
            last_around(1, "y", lambda c: (c, ALL, BOTH), cut_x, got)
        if splits[2]:
            got = [kept] + around(2, "x", lambda c: (at.y, c, at.z_hi), None, [])
            got = around(2, "y", lambda c: (c, ALL, at.z_hi), cut_x, got)
            across_both(2, got)
        if splits[3]:
            got = [kept] + around(3, "y", lambda c: (c, at.x, at.z_hi), None, [])
            got = around(3, "x", lambda c: (ALL, c, at.z_hi), cut_y, got)
            across_both(3, got)
        return found

    def mix(rows_ref, begin, weights, count, mask, write):
        rows = rows_ref[begin : begin + 256, :]
        width = rows.shape[1]
        step = width // 2
        for half in range(2):
            block = weights[2 * half : 2 * half + 2]
            mixed = lax.dot_general(
                rows,
                block.reshape(step, width),
                (((1,), (1,)), ((), ())),
                preferred_element_type=jnp.float32,
            )
            side = rows[:, half * step : (half + 1) * step].astype(jnp.float32)
            pred[:, half * step : (half + 1) * step] = side + mixed

        @pl.loop(0, 2)
        def _(i):
            spot = pl.ds(pl.multiple_of(i * 128, 128), 128)
            values = pred[spot, :width]
            write(spot, layer_norm(values, count, mask).astype(jnp.bfloat16))

    def dino():
        def write(spot, values):
            targets[0][spot, :] = values

        mix(held[0], 0, projs[0], 1536, None, write)

    def siglip():
        def write(spot, values):
            targets[1][spot, :] = values

        column = lax.broadcasted_iota(jnp.int32, (1, 1280), 1)
        mask = (column % 40 < 36).astype(jnp.float32)
        mix(held[1], 0, projs[1], 1152, mask, write)

    def sam(b):
        def run():
            def write(spot, values):
                cells[spot, :] = values

            mix(held[2], b * 256, projs[2], 1280, None, write)
            block = lax.broadcasted_iota(jnp.int32, (64, 256), 0)
            cell = lax.broadcasted_iota(jnp.int32, (64, 256), 1)
            member = ((cell >= 4 * block) & (cell < 4 * block + 4)).astype(jnp.bfloat16)
            total = jnp.dot(member, cells[...], preferred_element_type=jnp.float32)
            targets[2][b * 64 : b * 64 + 64, :] = (total * 0.25).astype(jnp.bfloat16)

        return run

    def pick(t):
        rows = rows_in[...].reshape(512, STUDENT)
        spot = lax.broadcasted_iota(jnp.int32, (256, 512), 0)
        source = lax.broadcasted_iota(jnp.int32, (256, 512), 1)
        column = at.z_hi * 8 + spot % 8
        straight = spot // 8 * 16 + column
        flags = jnp.dot(
            (source == straight).astype(jnp.bfloat16),
            rows[:, 1280:],
            preferred_element_type=jnp.float32,
        )
        shift = jnp.where(flags[:, t : t + 1] > 0.5, 0, 15 - 2 * column)
        normed[t][...] = jnp.dot(
            (source == straight + shift).astype(jnp.bfloat16),
            rows[:, :1280],
            preferred_element_type=jnp.float32,
        ).astype(jnp.bfloat16)

    def forward(t):
        def run():
            pick(t)
            act[...] = jnp.dot(
                normed[t][...],
                first_all[...].reshape(1280, 768),
                preferred_element_type=jnp.float32,
            )

            @pl.loop(0, 8)
            def _(i):
                spot = pl.ds(pl.multiple_of(i * 32, 32), 32)
                hid, tilt = gelu_pair(act[spot, :])
                hidden[t][spot, :] = hid.astype(jnp.bfloat16)
                slope[spot, :] = tilt

        return run

    def backward(t):
        width = WIDTHS[t]

        def run():
            second = second_all[:, :, :, :, :width].reshape(768, width)
            pred[:, :width] = jnp.dot(
                hidden[t][...], second, preferred_element_type=jnp.float32
            )

            @pl.loop(0, 8)
            def _(i):
                spot = pl.ds(pl.multiple_of(i * 32, 32), 32)
                wanted = targets[t][spot, :].astype(jnp.float32)
                grad = factor * (pred[spot, :width] - wanted)
                grad_pred[t][spot, :] = grad.astype(jnp.bfloat16)

            act[...] = lax.dot_general(
                grad_pred[t][...],
                second,
                (((1,), (1,)), ((), ())),
                preferred_element_type=jnp.float32,
            )

            @pl.loop(0, 8)
            def _(i):
                spot = pl.ds(pl.multiple_of(i * 32, 32), 32)
                grad_act[t][spot, :] = (act[spot, :] * slope[spot, :]).astype(jnp.bfloat16)

        return run

    def half_of(width, core):
        return pl.ds(pl.multiple_of(core * (width // 2), LANE), width // 2)

    def outer(left, right):
        return lax.dot_general(
            left, right, (((0,), (0,)), ((), ())), preferred_element_type=jnp.float32
        )

    def gradient(out, left, left_too, right, right_too):
        def run():
            mine, other = right[:, half_of(right.shape[1], at.core)], right_too[...]
            step = left.shape[1] // 2
            for side in range(2):
                columns = slice(step * side, step * side + step)
                total = outer(left[:, columns], mine) + outer(left_too[:, columns], other)
                out[2 * side : 2 * side + 2] = total.reshape((2,) + out.shape[1:])

        return run

    def reduce(k, splits, needs, rank):
        array = sums[k]
        depth = array.shape[3]

        def lanes(s):
            return pl.ds(sum(splits[:s]) * LANE, splits[s] * LANE)

        def view(s, region):
            return array.at[part(region[0]), part(region[1]), part(region[2]), :, lanes(s)]

        def send(s, region, link, device, needs):
            room = next(spare)

            def run():
                return copies.send(view(s, region), room, device)

            size = chunks(region) * depth * splits[s] * LANE * 4
            task = add_task(link, size, needs, run, rank)
            task.room = room
            return task

        def add(s, region, sent, needs):
            sizes = [extent(entry) for entry in region]

            def run():
                for spots in itertools.product(*[range(size or 1) for size in sizes]):
                    there = tuple(spot for spot, size in zip(spots, sizes) if size)
                    where = tuple(
                        spot + entry[0] if size else entry
                        for spot, size, entry in zip(spots, sizes, region)
                    ) + (slice(None), lanes(s))
                    total = array[where]
                    for task in sent:
                        total = total + task.room[there + (slice(None), slice(None))]
                    array[where] = total

            size = chunks(region) * depth * splits[s] * LANE * 4
            return add_task("core", 0.1 + size * 0.4e-6, sent + needs, run, -1)

        def across(s, needs):
            sent = send(s, (at.y, at.x, 1 - at.z_hi), "mirror", at.mirror_z(), needs)
            return [add(s, own, [sent], needs)]

        def across_both(s, needs):
            mine, other = (2 * at.z_lo, 2), (2 - 2 * at.z_lo, 2)
            sent = send(s, (other, ALL, 1 - at.z_hi), "next", at.next_z(), needs)
            added = add(s, (mine, ALL, 1 - at.z_hi), [sent], needs)
            sent = send(s, (mine, ALL, 1 - at.z_hi), "mirror", at.mirror_z(), [added])
            return [add(s, (other, ALL, at.z_hi), [sent], needs)]

        def around(s, axis, block, cut, needs):
            place, device = (at.x_at, at.x_next) if axis == "x" else (at.y_at, at.y_next)
            here, over, back, ahead = (block(place(step)) for step in (0, 2, -1, 1))
            up, down = [], []
            if cut is not None:
                sent = send(s, cut(over, 0), axis + "+", device(1), needs)
                up.append(add(s, cut(ahead, 0), [sent], needs))
                sent = send(s, cut(over, 1), axis + "-", device(-1), needs)
                down.append(add(s, cut(back, 1), [sent], needs))
            elif k % 2 == 0:
                sent = send(s, over, axis + "+", device(1), needs)
                up.append(add(s, ahead, [sent], needs))
            else:
                sent = send(s, over, axis + "-", device(-1), needs)
                down.append(add(s, back, [sent], needs))
            one = send(s, ahead, axis + "+", device(1), needs + up)
            two = send(s, back, axis + "-", device(-1), needs + down)
            return [add(s, here, [one, two], needs)]

        def settle(needs):
            def swap():
                return copies.send(array.at[own], last[k], at.next_z())

            def total():
                outs[k][at.core] = array[own] + last[k][...]

            def share_total():
                return copies.send(outs[k].at[at.core], outs[k].at[at.core], at.sibling())

            size = depth * sum(splits) * LANE * 4
            swapped = add_task("next", size, needs, swap, -1)
            added = add_task("core", 0.2, needs + [swapped], total, -1)
            add_task("sibling", size, [added], share_total, -1)

        done = []
        if splits[0]:
            got = around(0, "x", lambda c: (ALL, c, BOTH), cut_y, needs)
            got = around(0, "y", lambda c: (c, at.x, BOTH), cut_z, got)
            done += across(0, got)
        if splits[1]:
            got = around(1, "y", lambda c: (c, ALL, BOTH), cut_x, needs)
            got = around(1, "x", lambda c: (at.y, c, BOTH), cut_z, got)
            done += across(1, got)
        if splits[2]:
            got = across_both(2, needs)
            got = around(2, "y", lambda c: (c, ALL, at.z_hi), cut_x, got)
            done += around(2, "x", lambda c: (at.y, c, at.z_hi), None, got)
        if splits[3]:
            got = across_both(3, needs)
            got = around(3, "x", lambda c: (ALL, c, at.z_hi), cut_y, got)
            done += around(3, "y", lambda c: (c, at.x, at.z_hi), None, got)
        settle(done)

    loaded = [move(inputs[t], held[t], [], 10 * ORDER.index(t) + 3) for t in range(3)]
    rows_ready = None
    before = None
    for place, t in enumerate(ORDER):
        rank = 10 * place
        projected = gather(t, PROJ_SPLITS[t], rank)
        needs = projected + [loaded[t]]
        if t == 0:
            mapped = [add_task("core", 2.6, needs, dino, rank + 1)]
        elif t == 1:
            mapped = [add_task("core", 2.2, needs, siglip, rank + 1)]
        else:
            mapped = [add_task("core", 2.4, needs, sam(b), rank + 1) for b in range(4)]
        if rows_ready is None:
            rows_ready = spread_student()
        first = gather(3 + t, FIRST_SPLITS[t], rank + 1)
        second = gather(6 + t, SECOND_SPLITS[t], rank + 2)
        free = [before] if before else []
        ahead = [forwarded] if before else []
        first = move(whole[3 + t], first_all, first + ahead, rank)
        second = move(
            whole[6 + t], second_all.at[:, :, :, :, pl.ds(0, WIDTHS[t])], second + free, rank
        )
        forwarded = add_task("core", 3.0, [rows_ready, first] + free, forward(t), rank + 3)

        def share(src, dst, needs, rank=rank):
            if src.shape[1] != dst.shape[1]:
                src = src.at[:, half_of(src.shape[1], 1 - at.core)]
            return carry(src, dst, "sibling", at.sibling(), needs, rank)

        got_normed = share(normed[t], normed_too[t], [forwarded])
        got_hidden = share(hidden[t], hidden_too[t], [forwarded])
        before = add_task("core", 3.0, [second, forwarded] + mapped, backward(t), rank + 3)
        got_act = share(grad_act[t], grad_act_too[t], [before])
        got_pred = share(grad_pred[t], grad_pred_too[t], [before])
        run = gradient(sums[t], normed[t], normed_too[t], grad_act[t], grad_act_too[t])
        done = add_task("core", 1.6, [before, got_normed, got_act], run, rank + 2)
        reduce(t, GRAD_SPLITS[0][t], [done], 40 + place)
        run = gradient(sums[3 + t], hidden[t], hidden_too[t], grad_pred[t], grad_pred_too[t])
        done = add_task("core", 1.8, [before, got_hidden, got_pred], run, rank + 2)
        reduce(3 + t, GRAD_SPLITS[1][t], [done], 40 + place)
    carry_out(plan(tasks))
    copies.finish()


def distil(shards, inputs, student, factor):
    inside = pl.BlockSpec(memory_space=pltpu.VMEM)
    outside = pl.BlockSpec(memory_space=pl.ANY)
    depth = [40] * 3 + [24] * 3
    width = [384] * 3 + [w // 2 for w in WIDTHS]
    splits = GRAD_SPLITS[0] + GRAD_SPLITS[1]

    def rooms():
        plane, line = [(2, 2), (2, 2), (4, 2), (4, 2)], [(), (), (2,), (2,)]
        column, spot = [(2,), (2,), (4,), (4,)], [(), (), ()]
        leads = [plane + line + [()]] * 2 + [[(2, 4), (2, 4)] + column + spot] * 2
        for t in ORDER:
            for k in (t, 3 + t):
                for s in range(4):
                    if splits[k][s]:
                        for lead in leads[s]:
                            yield pltpu.VMEM(lead + (depth[k], splits[k][s] * LANE), jnp.float32)

    def half_wide(*shape):
        return jax.ShapeDtypeStruct(shape, jnp.bfloat16)

    def table(*shape):
        return pltpu.VMEM(shape, jnp.bfloat16)

    def three(*widths):
        return [table(256, w) for w in widths]

    outs = [jax.ShapeDtypeStruct((2, d, w), jnp.float32) for d, w in zip(depth, width)]
    landings = [half_wide(4, 4, 2, *shard.shape) for shard in shards[3:]] + [
        half_wide(2, 16, STUDENT),
        half_wide(2, 16, STUDENT),
        half_wide(4, 4, 16, STUDENT),
        half_wide(2, 16, STUDENT),
        half_wide(2, 16, STUDENT),
        half_wide(4, 4, 2, 16, STUDENT),
        half_wide(2, 4, 16, STUDENT),
        half_wide(2, 4, 16, STUDENT),
    ]
    results = pl.pallas_call(
        functools.partial(kernel, factor),
        out_shape=outs + landings,
        in_specs=[outside] * (len(shards) + len(inputs) + 1),
        out_specs=[inside] * len(outs) + [outside] * len(landings),
        scratch_shapes=[
            table(4, 4, 2, 48, 1536),
            table(4, 4, 2, 40, 1280),
            table(4, 4, 2, 40, 1280),
            table(4, 4, 2, 40, 768),
            table(4, 4, 2, 24, 1536),
            table(4, 4, 2, 16, STUDENT),
            *[table(*rows.shape) for rows in inputs],
            *three(*WIDTHS),
            table(256, 1280),
            pltpu.VMEM((256, 768), jnp.float32),
            pltpu.VMEM((256, 1536), jnp.float32),
            pltpu.VMEM((256, 768), jnp.float32),
            *three(*[1280] * 6),
            *three(*[768] * 6),
            *three(*[768] * 3),
            *three(*[384] * 3),
            *three(*WIDTHS),
            *three(*[w // 2 for w in WIDTHS]),
            *[pltpu.VMEM((4, 4, 2, d, w), jnp.float32) for d, w in zip(depth, width)],
            *[pltpu.VMEM((d, w), jnp.float32) for d, w in zip(depth, width)],
            *rooms(),
            pltpu.SemaphoreType.DMA((LOCALS,)),
            pltpu.SemaphoreType.DMA((SENDS,)),
            pltpu.SemaphoreType.DMA((COPIES,)),
        ],
        compiler_params=pltpu.CompilerParams(
            collective_id=0, has_side_effects=True, vmem_limit_bytes=63 * 1024 * 1024
        ),
        name="distil",
    )(*shards, *inputs, student)
    return results[: len(outs)]


def spread(width, group, room):
    rows = lax.broadcasted_iota(jnp.int32, (width, width // group * room), 0)
    columns = lax.broadcasted_iota(jnp.int32, (width, width // group * room), 1)
    return (rows // group * room + rows % group == columns).astype(jnp.bfloat16)


def place_columns(values, table):
    return jnp.dot(values, table, preferred_element_type=jnp.float32).astype(jnp.bfloat16)


def student_rows(student_feats, indices):
    normed = layer_norm(student_feats[0].astype(jnp.float32)).astype(jnp.bfloat16)
    patches = jnp.arange(256, dtype=jnp.int32)
    flags = jnp.stack([index[0] == patches for index in indices], axis=-1).astype(jnp.bfloat16)
    rows = jnp.concatenate([normed, jnp.pad(flags, ((0, 0), (0, LANE - 3)))], axis=-1)
    return rows.reshape(4, 4, 16, STUDENT)


def body(
    student_feats,
    dino_in,
    siglip_in,
    sam_in,
    dino_proj,
    siglip_proj,
    sam_proj,
    dino_index,
    siglip_index,
    sam_index,
    dino_first,
    dino_second,
    siglip_first,
    siglip_second,
    sam_first,
    sam_second,
):
    images_total = student_feats.shape[0] * 128
    siglip_room = spread(1152, 36, 40)
    hidden_room = spread(640, 20, 24)
    siglip_turned = jnp.pad(place_columns(siglip_proj.T, siglip_room), ((0, 4), (0, 0)))
    firsts = place_columns(
        jnp.concatenate([dino_first, siglip_first, sam_first], axis=0), hidden_room
    ).reshape(3, 40, 768)
    seconds = [
        jnp.pad(second, ((0, 4), (0, 0)))
        for second in (dino_second, place_columns(siglip_second, siglip_room), sam_second)
    ]
    sums = distil(
        [dino_proj.T, siglip_turned, sam_proj.T, *firsts, *seconds],
        [
            dino_in.reshape(256, -1),
            place_columns(siglip_in.reshape(256, -1), siglip_room),
            sam_in.reshape(1024, -1),
        ],
        student_rows(student_feats, (dino_index, siglip_index, sam_index)),
        2.0 / images_total,
    )
    joined = [jnp.concatenate([total[0], total[1]], axis=-1) for total in sums]
    firsts = [total.reshape(40, 32, 24)[..., :20].reshape(40, 640) for total in joined[:3]]
    seconds = [total[:20] for total in joined[3:]]
    siglip_two = seconds[1].reshape(20, 32, 40)[..., :36].reshape(20, 1152)
    return (firsts[0], seconds[0], firsts[1], siglip_two, firsts[2], seconds[2])


def solution(mesh):
    shared = P("wide", None)
    return jax.shard_map(
        body,
        mesh=mesh,
        in_specs=(
            P(("grp", "wide"), None, None),
            *[P("grp", "wide", None)] * 3,
            *[P(None, "wide")] * 3,
            *[P(("grp", "wide"), None)] * 3,
            *[shared] * 6,
        ),
        out_specs=(shared,) * 6,
        check_vma=False,
    )
```

```python
import functools
import itertools
import math

import jax
import jax.numpy as jnp
from jax import lax
from jax.experimental import pallas as pl
from jax.experimental.pallas import tpu as pltpu
from jax.sharding import PartitionSpec as P

MESH = pl.DeviceIdType.MESH
LANE = 128
ALL = (0, 4)
BOTH = (0, 2)


def layer_norm(values, count=None, mask=None):
    count = values.shape[-1] if count is None else count
    centered = values - jnp.sum(values, axis=-1, keepdims=True) * (1.0 / count)
    if mask is not None:
        centered = centered * mask
    variance = jnp.sum(centered * centered, axis=-1, keepdims=True) * (1.0 / count)
    return centered * lax.rsqrt(variance + 1e-05)


def gelu_pair(act):
    cdf = 0.5 * (1.0 + jax.scipy.special.erf(act * (1.0 / math.sqrt(2.0))))
    density = jnp.exp(-0.5 * act * act) * (1.0 / math.sqrt(2.0 * math.pi))
    return (act * cdf, cdf + act * density)


class Place:
    def __init__(self):
        grp, wide = lax.axis_index("grp"), lax.axis_index("wide")
        self.grp, self.wide = grp, wide
        self.z_lo, self.core = grp // 2, grp % 2
        self.y, self.x, self.z_hi = wide // 8, wide // 2 % 4, wide % 2

    def x_next(self, step):
        return (self.grp, (self.y * 4 + self.x_at(step)) * 2 + self.z_hi)

    def y_next(self, step):
        return (self.grp, (self.y_at(step) * 4 + self.x) * 2 + self.z_hi)

    def x_at(self, step):
        return (self.x + step + 4) % 4

    def y_at(self, step):
        return (self.y + step + 4) % 4

    def mirror_z(self):
        return ((1 - self.z_lo) * 2 + self.core, (self.y * 4 + self.x) * 2 + 1 - self.z_hi)

    def next_z(self):
        return ((1 - self.z_lo) * 2 + self.core, self.wide)

    def sibling(self):
        return (self.z_lo * 2 + 1 - self.core, self.wide)


def enter(partners):
    barrier = pltpu.get_barrier_semaphore()
    for partner in partners:
        pl.semaphore_signal(barrier, inc=1, device_id=partner, device_id_type=MESH)
    pl.semaphore_wait(barrier, len(partners))


def part(entry):
    return pl.ds(entry[0], entry[1]) if isinstance(entry, tuple) else entry


def extent(entry):
    return entry[1] if isinstance(entry, tuple) else None


class Copies:
    def __init__(self, send_sem, recv_sem):
        self.send_sem, self.recv_sem = send_sem, recv_sem
        self.started = []

    def send(self, src, dst, device):
        i = len(self.started)
        if i >= SENDS:
            self.started[i - SENDS].wait_send()
        copy = pltpu.make_async_remote_copy(
            src_ref=src,
            dst_ref=dst,
            send_sem=self.send_sem.at[i % SENDS],
            recv_sem=self.recv_sem.at[i],
            device_id=device,
            device_id_type=MESH,
        )
        copy.start()
        self.started.append(copy)
        return copy

    def finish(self):
        for copy in self.started[-SENDS:]:
            copy.wait_send()


class Task:
    def __init__(self, link, cost, needs, run, rank=0):
        self.link, self.cost, self.run, self.rank = link, cost, run, rank
        self.needs = [need for need in needs if need is not None]
        self.copy, self.landed, self.done = None, False, None


BACKLOG = 2.0
LATENCY = 3.0
RATES = {"sibling": 0.4, "local": 0.65}


def span(task):
    return task.cost if task.link == "core" else task.cost * 1e-6 / RATES.get(task.link, 0.0445)


def plan(tasks):
    tails = {id(task): 0.0 for task in tasks}
    for task in reversed(tasks):
        tail = tails[id(task)] + span(task) + (0.0 if task.link == "core" else 1.5)
        for need in task.needs:
            tails[id(need)] = max(tails[id(need)], tail)
    free, now, order, left = {}, 0.0, [], list(tasks)
    while left:
        best = None
        for task in left:
            ready = 0.0
            for need in task.needs:
                if need.done is None:
                    break
                ready = max(ready, need.done)
            else:
                if task.link != "core":
                    ready = max(ready, free.get(task.link, 0.0) - BACKLOG)
                key = (max(ready, now), task.link == "core", task.rank, -tails[id(task)])
                if best is None or key < best[0]:
                    best = (key, task)
        (now, *_), task = best
        if task.link == "core":
            now += task.cost
            task.done = now
        else:
            now += 0.03
            free[task.link] = max(now, free.get(task.link, 0.0)) + span(task)
            task.done = free[task.link] + LATENCY
        order.append(task)
        left.remove(task)
    return order


def carry_out(order):
    for task in order:
        for need in task.needs:
            land(need)
        task.copy = task.run()
    for task in order:
        land(task)


def land(task):
    if task.copy is not None and not task.landed:
        if task.link == "local":
            task.copy.wait()
        else:
            task.copy.wait_recv()
        task.landed = True


WIDTHS = (1536, 1280, 1280)
STUDENT = 1280 + LANE
PROJ_SPLITS = ((2, 1, 2, 1), (1, 2, 1, 1), (1, 1, 1, 2))
FIRST_SPLITS = ((1, 1, 1, 0), (1, 1, 0, 1), (1, 0, 1, 1))
SECOND_SPLITS = ((1, 2, 1, 2), (1, 1, 2, 1), (1, 2, 1, 1))
GRAD_SPLITS = (
    ((1, 0, 1, 1), (0, 1, 1, 1), (1, 1, 1, 0)),
    ((1, 1, 2, 2), (1, 1, 1, 2), (1, 1, 2, 1)),
)
COPIES = 646
SENDS = 48
ORDER = (2, 0, 1)
EARLY = 1
LOCALS = 24


def cut_y(region, half):
    return ((half * 2, 2), region[1], region[2])


def cut_x(region, half):
    return (region[0], (half * 2, 2), region[2])


def cut_z(region, half):
    return (region[0], region[1], half)


def chunks(region):
    return math.prod(extent(entry) or 1 for entry in region)


class Refs:
    def __init__(self, refs):
        self.refs = list(refs)

    def take(self, count):
        taken, self.refs = self.refs[:count], self.refs[count:]
        return taken


def kernel(factor, *refs):
    refs = Refs(refs)
    shards, inputs, (feats, flags_in) = refs.take(9), refs.take(3), refs.take(2)
    outs, weights = refs.take(6), refs.take(6)
    hop_y, ((rows_y,), hop_x, (rows_all,), hop_z) = refs.take(2), (
        refs.take(1),
        refs.take(2),
        refs.take(1),
        refs.take(2),
    )
    projs, (first_all, second_all, rows_in) = refs.take(3), refs.take(3)
    whole = projs + weights
    held, targets = refs.take(3), refs.take(3)
    (act, pred, slope) = refs.take(3)
    normed, normed_too, hidden, hidden_too = (refs.take(3) for _ in range(4))
    grad_act, grad_act_too, grad_pred, grad_pred_too = (refs.take(3) for _ in range(4))
    cells = grad_pred[2]
    sums, last = refs.take(6), refs.take(6)
    (student_in,) = refs.take(1)
    spare, (local_sem, send_sem, recv_sem) = iter(refs.refs[:-3]), refs.refs[-3:]
    at = Place()
    student_in[:, :, :, :1280] = (
        layer_norm(feats[...].astype(jnp.float32))
        .astype(jnp.bfloat16)
        .reshape(4, 4, 16, 1280)
    )
    student_in[:, :, :, 1280:] = flags_in[...].reshape(4, 4, 16, LANE)
    enter(
        [
            at.x_next(1),
            at.x_next(-1),
            at.y_next(1),
            at.y_next(-1),
            at.mirror_z(),
            at.next_z(),
            at.sibling(),
        ]
    )
    copies = Copies(send_sem, recv_sem)
    locals_used = itertools.count()
    tasks = []
    own = (at.y, at.x, at.z_hi)

    def add_task(*args):
        tasks.append(Task(*args))
        return tasks[-1]

    def size_of(ref):
        return math.prod(ref.shape) * 2

    def move(src, dst, needs, rank):
        def run():
            copy = pltpu.make_async_copy(src, dst, local_sem.at[next(locals_used)])
            copy.start()
            return copy

        return add_task("local", size_of(dst), needs, run, rank)

    def carry(src, dst, link, device, needs, rank):
        def run():
            return copies.send(src, dst, device)

        return add_task(link, size_of(dst), needs, run, rank)

    def spread_student():
        x_low, x_high = pl.ds(0, 2), pl.ds(2, 2)
        here = move(student_in.at[at.y], rows_y.at[at.y], [], EARLY)
        got = [here]
        got.append(
            carry(student_in.at[at.y_at(1)], rows_y.at[at.y], "y+", at.y_next(1), [], EARLY)
        )
        got.append(
            carry(student_in.at[at.y_at(-1)], rows_y.at[at.y], "y-", at.y_next(-1), [], EARLY)
        )
        far = student_in.at[at.y_at(2)]
        up = carry(far.at[x_low], hop_y[0], "y+", at.y_next(1), [], EARLY)
        down = carry(far.at[x_high], hop_y[1], "y-", at.y_next(-1), [], EARLY)
        got.append(
            carry(hop_y[0], rows_y.at[at.y_at(-1), x_low], "y+", at.y_next(1), [up], EARLY)
        )
        got.append(
            carry(hop_y[1], rows_y.at[at.y_at(1), x_high], "y-", at.y_next(-1), [down], EARLY)
        )

        every, low, high = pl.ds(0, 4), pl.ds(0, 2), pl.ds(2, 2)
        mine = rows_all.at[every, at.x, at.z_hi]
        done = [move(rows_y.at[every, at.x], mine, got, EARLY)]
        for step, link in ((1, "x+"), (-1, "x-")):
            src = rows_y.at[every, at.x_at(step)]
            done.append(carry(src, mine, link, at.x_next(step), got, EARLY))
        far = at.x_at(2)
        up = carry(rows_y.at[low, far], hop_x[0], "x+", at.x_next(1), got, EARLY)
        down = carry(rows_y.at[high, far], hop_x[1], "x-", at.x_next(-1), got, EARLY)
        dst = rows_all.at[low, at.x_at(-1), at.z_hi]
        done.append(carry(hop_x[0], dst, "x+", at.x_next(1), [up], EARLY))
        dst = rows_all.at[high, at.x_at(1), at.z_hi]
        done.append(carry(hop_x[1], dst, "x-", at.x_next(-1), [down], EARLY))

        landed = []
        for i in range(2):
            one, two = pl.ds(i, 1), pl.ds(2 + i, 1)
            src = rows_all.at[one, every, at.z_hi]
            first = carry(src, hop_z[0].at[one], "mirror", at.mirror_z(), done, EARLY)
            src = rows_all.at[two, every, at.z_hi]
            second = carry(src, hop_z[1].at[one], "next", at.next_z(), done, EARLY)
            dst = rows_all.at[one, every, 1 - at.z_hi]
            src = hop_z[0].at[one]
            landed.append(carry(src, dst, "next", at.next_z(), [first], EARLY))
            dst = rows_all.at[two, every, at.z_hi]
            src = hop_z[1].at[one]
            landed.append(carry(src, dst, "mirror", at.mirror_z(), [second], EARLY))
        return move(rows_all, rows_in, done + landed, EARLY)

    def gather(k, splits, rank):
        shard, array = shards[k], whole[k]
        found = []

        def lanes(s):
            start = at.core * sum(splits) + sum(splits[:s])
            return pl.ds(pl.multiple_of(start * LANE, LANE), splits[s] * LANE)

        def view(s, region):
            return array.at[part(region[0]), part(region[1]), part(region[2]), :, lanes(s)]

        def send(s, region, link, device, needs):
            src = shard.at[:, lanes(s)] if region is own else view(s, region)
            return carry(src, view(s, region), link, device, needs, rank)

        def share(s, region, needs):
            found.append(send(s, region, "sibling", at.sibling(), needs))

        def across(s):
            return [kept, send(s, own, "mirror", at.mirror_z(), [])]

        def across_both(s, needs):
            mine, other = (2 * at.z_lo, 2), (2 - 2 * at.z_lo, 2)
            share(s, (ALL, ALL, at.z_hi), needs)
            one = send(s, (other, ALL, at.z_hi), "mirror", at.mirror_z(), needs)
            two = send(s, (mine, ALL, 1 - at.z_hi), "next", at.next_z(), [one])
            share(s, (mine, ALL, 1 - at.z_hi), [one])
            share(s, (other, ALL, 1 - at.z_hi), [two])
            found.extend(needs + [one, two])

        def last_around(s, axis, block, cut, needs):
            place = at.x_at if axis == "x" else at.y_at
            share(s, block(place(0)), needs)
            up, down, one, two = around(s, axis, block, cut, needs)[len(needs) :]
            share(s, block(place(-1)), [up])
            share(s, block(place(1)), [down])
            share(s, block(place(2)), [one, two])
            found.extend(needs + [up, down, one, two])

        def around(s, axis, block, cut, needs):
            place, device = (at.x_at, at.x_next) if axis == "x" else (at.y_at, at.y_next)
            here = own if cut is None else block(place(0))
            back, ahead = block(place(-1)), block(place(1))
            up = send(s, here, axis + "+", device(1), needs)
            down = send(s, here, axis + "-", device(-1), needs)
            got = needs + [up, down]
            if cut is not None:
                got.append(send(s, cut(back, 0), axis + "+", device(1), [up]))
                got.append(send(s, cut(ahead, 1), axis + "-", device(-1), [down]))
            elif k % 2 == 0:
                got.append(send(s, back, axis + "+", device(1), [up]))
            else:
                got.append(send(s, ahead, axis + "-", device(-1), [down]))
            return got

        def keep():
            start = pl.multiple_of(at.core * sum(splits) * LANE, LANE)
            columns = pl.ds(start, sum(splits) * LANE)
            return move(shard.at[:, columns], array.at[own + (slice(None), columns)], [], -1)

        kept = keep()
        found.append(kept)
        if splits[0]:
            got = around(0, "y", lambda c: (c, at.x, BOTH), cut_z, across(0))
            last_around(0, "x", lambda c: (ALL, c, BOTH), cut_y, got)
        if splits[1]:
            got = around(1, "x", lambda c: (at.y, c, BOTH), cut_z, across(1))
            last_around(1, "y", lambda c: (c, ALL, BOTH), cut_x, got)
        if splits[2]:
            got = [kept] + around(2, "x", lambda c: (at.y, c, at.z_hi), None, [])
            got = around(2, "y", lambda c: (c, ALL, at.z_hi), cut_x, got)
            across_both(2, got)
        if splits[3]:
            got = [kept] + around(3, "y", lambda c: (c, at.x, at.z_hi), None, [])
            got = around(3, "x", lambda c: (ALL, c, at.z_hi), cut_y, got)
            across_both(3, got)
        return found

    def mix(rows_ref, begin, weights, count, mask, write):
        rows = rows_ref[begin : begin + 256, :]
        width = rows.shape[1]
        step = width // 2
        for half in range(2):
            block = weights[2 * half : 2 * half + 2]
            mixed = lax.dot_general(
                rows,
                block.reshape(step, width),
                (((1,), (1,)), ((), ())),
                preferred_element_type=jnp.float32,
            )
            side = rows[:, half * step : (half + 1) * step].astype(jnp.float32)
            pred[:, half * step : (half + 1) * step] = side + mixed

        @pl.loop(0, 2)
        def _(i):
            spot = pl.ds(pl.multiple_of(i * 128, 128), 128)
            values = pred[spot, :width]
            write(spot, layer_norm(values, count, mask).astype(jnp.bfloat16))

    def dino():
        def write(spot, values):
            targets[0][spot, :] = values

        mix(held[0], 0, projs[0], 1536, None, write)

    def siglip():
        def write(spot, values):
            targets[1][spot, :] = values

        column = lax.broadcasted_iota(jnp.int32, (1, 1280), 1)
        mask = (column % 40 < 36).astype(jnp.float32)
        mix(held[1], 0, projs[1], 1152, mask, write)

    def sam(b):
        def run():
            def write(spot, values):
                cells[spot, :] = values

            mix(held[2], b * 256, projs[2], 1280, None, write)
            block = lax.broadcasted_iota(jnp.int32, (64, 256), 0)
            cell = lax.broadcasted_iota(jnp.int32, (64, 256), 1)
            member = ((cell >= 4 * block) & (cell < 4 * block + 4)).astype(jnp.bfloat16)
            total = jnp.dot(member, cells[...], preferred_element_type=jnp.float32)
            targets[2][b * 64 : b * 64 + 64, :] = (total * 0.25).astype(jnp.bfloat16)

        return run

    def pick(t):
        rows = rows_in[...].reshape(512, STUDENT)
        spot = lax.broadcasted_iota(jnp.int32, (256, 512), 0)
        source = lax.broadcasted_iota(jnp.int32, (256, 512), 1)
        column = at.z_hi * 8 + spot % 8
        straight = spot // 8 * 16 + column
        flags = jnp.dot(
            (source == straight).astype(jnp.bfloat16),
            rows[:, 1280:],
            preferred_element_type=jnp.float32,
        )
        shift = jnp.where(flags[:, t : t + 1] > 0.5, 0, 15 - 2 * column)
        normed[t][...] = jnp.dot(
            (source == straight + shift).astype(jnp.bfloat16),
            rows[:, :1280],
            preferred_element_type=jnp.float32,
        ).astype(jnp.bfloat16)

    def forward(t):
        def run():
            pick(t)
            act[...] = jnp.dot(
                normed[t][...],
                first_all[...].reshape(1280, 768),
                preferred_element_type=jnp.float32,
            )

            @pl.loop(0, 8)
            def _(i):
                spot = pl.ds(pl.multiple_of(i * 32, 32), 32)
                hid, tilt = gelu_pair(act[spot, :])
                hidden[t][spot, :] = hid.astype(jnp.bfloat16)
                slope[spot, :] = tilt

        return run

    def backward(t):
        width = WIDTHS[t]

        def run():
            second = second_all[:, :, :, :, :width].reshape(768, width)
            pred[:, :width] = jnp.dot(
                hidden[t][...], second, preferred_element_type=jnp.float32
            )

            @pl.loop(0, 8)
            def _(i):
                spot = pl.ds(pl.multiple_of(i * 32, 32), 32)
                wanted = targets[t][spot, :].astype(jnp.float32)
                grad = factor * (pred[spot, :width] - wanted)
                grad_pred[t][spot, :] = grad.astype(jnp.bfloat16)

            act[...] = lax.dot_general(
                grad_pred[t][...],
                second,
                (((1,), (1,)), ((), ())),
                preferred_element_type=jnp.float32,
            )

            @pl.loop(0, 8)
            def _(i):
                spot = pl.ds(pl.multiple_of(i * 32, 32), 32)
                grad_act[t][spot, :] = (act[spot, :] * slope[spot, :]).astype(jnp.bfloat16)

        return run

    def half_of(width, core):
        return pl.ds(pl.multiple_of(core * (width // 2), LANE), width // 2)

    def outer(left, right):
        return lax.dot_general(
            left, right, (((0,), (0,)), ((), ())), preferred_element_type=jnp.float32
        )

    def gradient(out, left, left_too, right, right_too):
        def run():
            mine, other = right[:, half_of(right.shape[1], at.core)], right_too[...]
            step = left.shape[1] // 2
            for side in range(2):
                columns = slice(step * side, step * side + step)
                total = outer(left[:, columns], mine) + outer(left_too[:, columns], other)
                out[2 * side : 2 * side + 2] = total.reshape((2,) + out.shape[1:])

        return run

    def reduce(k, splits, needs, rank):
        array = sums[k]
        depth = array.shape[3]

        def lanes(s):
            return pl.ds(sum(splits[:s]) * LANE, splits[s] * LANE)

        def view(s, region):
            return array.at[part(region[0]), part(region[1]), part(region[2]), :, lanes(s)]

        def send(s, region, link, device, needs):
            room = next(spare)

            def run():
                return copies.send(view(s, region), room, device)

            size = chunks(region) * depth * splits[s] * LANE * 4
            task = add_task(link, size, needs, run, rank)
            task.room = room
            return task

        def add(s, region, sent, needs):
            sizes = [extent(entry) for entry in region]

            def run():
                for spots in itertools.product(*[range(size or 1) for size in sizes]):
                    there = tuple(spot for spot, size in zip(spots, sizes) if size)
                    where = tuple(
                        spot + entry[0] if size else entry
                        for spot, size, entry in zip(spots, sizes, region)
                    ) + (slice(None), lanes(s))
                    total = array[where]
                    for task in sent:
                        total = total + task.room[there + (slice(None), slice(None))]
                    array[where] = total

            size = chunks(region) * depth * splits[s] * LANE * 4
            return add_task("core", 0.03 + size * 0.06e-6, sent + needs, run, -1)

        def across(s, needs):
            sent = send(s, (at.y, at.x, 1 - at.z_hi), "mirror", at.mirror_z(), needs)
            return [add(s, own, [sent], needs)]

        def across_both(s, needs):
            mine, other = (2 * at.z_lo, 2), (2 - 2 * at.z_lo, 2)
            sent = send(s, (other, ALL, 1 - at.z_hi), "next", at.next_z(), needs)
            added = add(s, (mine, ALL, 1 - at.z_hi), [sent], needs)
            sent = send(s, (mine, ALL, 1 - at.z_hi), "mirror", at.mirror_z(), [added])
            return [add(s, (other, ALL, at.z_hi), [sent], needs)]

        def around(s, axis, block, cut, needs):
            place, device = (at.x_at, at.x_next) if axis == "x" else (at.y_at, at.y_next)
            here, over, back, ahead = (block(place(step)) for step in (0, 2, -1, 1))
            up, down = [], []
            if cut is not None:
                sent = send(s, cut(over, 0), axis + "+", device(1), needs)
                up.append(add(s, cut(ahead, 0), [sent], needs))
                sent = send(s, cut(over, 1), axis + "-", device(-1), needs)
                down.append(add(s, cut(back, 1), [sent], needs))
            elif k % 2 == 0:
                sent = send(s, over, axis + "+", device(1), needs)
                up.append(add(s, ahead, [sent], needs))
            else:
                sent = send(s, over, axis + "-", device(-1), needs)
                down.append(add(s, back, [sent], needs))
            one = send(s, ahead, axis + "+", device(1), needs + up)
            two = send(s, back, axis + "-", device(-1), needs + down)
            return [add(s, here, [one, two], needs)]

        def settle(needs):
            mine = half_of(outs[k].shape[1], at.core)

            def swap():
                return copies.send(array.at[own], last[k], at.next_z())

            def total():
                outs[k][:, mine] = array[own] + last[k][...]

            def share_total():
                return copies.send(outs[k].at[:, mine], outs[k].at[:, mine], at.sibling())

            size = depth * sum(splits) * LANE * 4
            swapped = add_task("next", size, needs, swap, -1)
            added = add_task("core", 0.1, needs + [swapped], total, -1)
            add_task("sibling", size, [added], share_total, -1)

        done = []
        if splits[0]:
            got = around(0, "x", lambda c: (ALL, c, BOTH), cut_y, needs)
            got = around(0, "y", lambda c: (c, at.x, BOTH), cut_z, got)
            done += across(0, got)
        if splits[1]:
            got = around(1, "y", lambda c: (c, ALL, BOTH), cut_x, needs)
            got = around(1, "x", lambda c: (at.y, c, BOTH), cut_z, got)
            done += across(1, got)
        if splits[2]:
            got = across_both(2, needs)
            got = around(2, "y", lambda c: (c, ALL, at.z_hi), cut_x, got)
            done += around(2, "x", lambda c: (at.y, c, at.z_hi), None, got)
        if splits[3]:
            got = across_both(3, needs)
            got = around(3, "x", lambda c: (ALL, c, at.z_hi), cut_y, got)
            done += around(3, "y", lambda c: (c, at.x, at.z_hi), None, got)
        settle(done)

    loaded = [move(inputs[t], held[t], [], 10 * ORDER.index(t) + 3) for t in range(3)]
    rows_ready = None
    before = None
    for place, t in enumerate(ORDER):
        rank = 10 * place
        projected = gather(t, PROJ_SPLITS[t], rank)
        needs = projected + [loaded[t]]
        if t == 0:
            mapped = [add_task("core", 2.0, needs, dino, rank + 1)]
        elif t == 1:
            mapped = [add_task("core", 1.7, needs, siglip, rank + 1)]
        else:
            mapped = [add_task("core", 1.8, needs, sam(b), rank + 1) for b in range(4)]
        if rows_ready is None:
            rows_ready = spread_student()
        first = gather(3 + t, FIRST_SPLITS[t], rank + 1)
        second = gather(6 + t, SECOND_SPLITS[t], rank + 2)
        free = [before] if before else []
        ahead = [forwarded] if before else []
        first = move(whole[3 + t], first_all, first + ahead, rank)
        second = move(
            whole[6 + t], second_all.at[:, :, :, :, pl.ds(0, WIDTHS[t])], second + free, rank
        )
        forwarded = add_task("core", 2.1, [rows_ready, first] + free, forward(t), rank + 3)

        def share(src, dst, needs, rank=rank):
            if src.shape[1] != dst.shape[1]:
                src = src.at[:, half_of(src.shape[1], 1 - at.core)]
            return carry(src, dst, "sibling", at.sibling(), needs, rank)

        got_normed = share(normed[t], normed_too[t], [forwarded])
        got_hidden = share(hidden[t], hidden_too[t], [forwarded])
        before = add_task("core", 2.1, [second, forwarded] + mapped, backward(t), rank + 3)
        got_act = share(grad_act[t], grad_act_too[t], [before])
        got_pred = share(grad_pred[t], grad_pred_too[t], [before])
        run = gradient(sums[t], normed[t], normed_too[t], grad_act[t], grad_act_too[t])
        done = add_task("core", 0.6, [before, got_normed, got_act], run, rank + 2)
        reduce(t, GRAD_SPLITS[0][t], [done], 40 + place)
        run = gradient(sums[3 + t], hidden[t], hidden_too[t], grad_pred[t], grad_pred_too[t])
        done = add_task("core", 0.7, [before, got_hidden, got_pred], run, rank + 2)
        reduce(3 + t, GRAD_SPLITS[1][t], [done], 40 + place)
    carry_out(plan(tasks))
    copies.finish()


def distil(shards, inputs, feats, flags, factor):
    inside = pl.BlockSpec(memory_space=pltpu.VMEM)
    outside = pl.BlockSpec(memory_space=pl.ANY)
    depth = [40] * 3 + [24] * 3
    width = [384] * 3 + [w // 2 for w in WIDTHS]
    splits = GRAD_SPLITS[0] + GRAD_SPLITS[1]

    def rooms():
        plane, line = [(2, 2), (2, 2), (4, 2), (4, 2)], [(), (), (2,), (2,)]
        column, spot = [(2,), (2,), (4,), (4,)], [(), (), ()]
        leads = [plane + line + [()]] * 2 + [[(2, 4), (2, 4)] + column + spot] * 2
        for t in ORDER:
            for k in (t, 3 + t):
                for s in range(4):
                    if splits[k][s]:
                        for lead in leads[s]:
                            yield pltpu.VMEM(lead + (depth[k], splits[k][s] * LANE), jnp.float32)

    def half_wide(*shape):
        return jax.ShapeDtypeStruct(shape, jnp.bfloat16)

    def table(*shape):
        return pltpu.VMEM(shape, jnp.bfloat16)

    def three(*widths):
        return [table(256, w) for w in widths]

    outs = [jax.ShapeDtypeStruct((d, 2 * w), jnp.float32) for d, w in zip(depth, width)]
    landings = [half_wide(4, 4, 2, *shard.shape) for shard in shards[3:]] + [
        half_wide(2, 16, STUDENT),
        half_wide(2, 16, STUDENT),
        half_wide(4, 4, 16, STUDENT),
        half_wide(2, 16, STUDENT),
        half_wide(2, 16, STUDENT),
        half_wide(4, 4, 2, 16, STUDENT),
        half_wide(2, 4, 16, STUDENT),
        half_wide(2, 4, 16, STUDENT),
    ]
    results = pl.pallas_call(
        functools.partial(kernel, factor),
        out_shape=outs + landings,
        in_specs=[outside] * (len(shards) + len(inputs)) + [inside] * 2,
        out_specs=[inside] * len(outs) + [outside] * len(landings),
        scratch_shapes=[
            table(4, 4, 2, 48, 1536),
            table(4, 4, 2, 40, 1280),
            table(4, 4, 2, 40, 1280),
            table(4, 4, 2, 40, 768),
            table(4, 4, 2, 24, 1536),
            table(4, 4, 2, 16, STUDENT),
            *[table(*rows.shape) for rows in inputs],
            *three(*WIDTHS),
            pltpu.VMEM((256, 768), jnp.float32),
            pltpu.VMEM((256, 1536), jnp.float32),
            pltpu.VMEM((256, 768), jnp.float32),
            *three(*[1280] * 6),
            *three(*[768] * 6),
            *three(*[768] * 3),
            *three(*[384] * 3),
            *three(*WIDTHS),
            *three(*[w // 2 for w in WIDTHS]),
            *[pltpu.VMEM((4, 4, 2, d, w), jnp.float32) for d, w in zip(depth, width)],
            *[pltpu.VMEM((d, w), jnp.float32) for d, w in zip(depth, width)],
            table(4, 4, 16, STUDENT),
            *rooms(),
            pltpu.SemaphoreType.DMA((LOCALS,)),
            pltpu.SemaphoreType.DMA((SENDS,)),
            pltpu.SemaphoreType.DMA((COPIES,)),
        ],
        compiler_params=pltpu.CompilerParams(
            collective_id=0, has_side_effects=True, vmem_limit_bytes=63 * 1024 * 1024
        ),
        name="distil",
    )(*shards, *inputs, feats, flags)
    return results[: len(outs)]


def spread(width, group, room):
    rows = lax.broadcasted_iota(jnp.int32, (width, width // group * room), 0)
    columns = lax.broadcasted_iota(jnp.int32, (width, width // group * room), 1)
    return (rows // group * room + rows % group == columns).astype(jnp.bfloat16)


def place_columns(values, table):
    return jnp.dot(values, table, preferred_element_type=jnp.float32).astype(jnp.bfloat16)


def mirror_flags(indices):
    patches = jnp.arange(256, dtype=jnp.int32)
    flags = jnp.stack([index[0] == patches for index in indices], axis=-1).astype(jnp.bfloat16)
    return jnp.pad(flags, ((0, 0), (0, LANE - 3)))


def body(
    student_feats,
    dino_in,
    siglip_in,
    sam_in,
    dino_proj,
    siglip_proj,
    sam_proj,
    dino_index,
    siglip_index,
    sam_index,
    dino_first,
    dino_second,
    siglip_first,
    siglip_second,
    sam_first,
    sam_second,
):
    images_total = student_feats.shape[0] * 128
    siglip_room = spread(1152, 36, 40)
    hidden_room = spread(640, 20, 24)
    siglip_turned = jnp.pad(place_columns(siglip_proj.T, siglip_room), ((0, 4), (0, 0)))
    firsts = place_columns(
        jnp.concatenate([dino_first, siglip_first, sam_first], axis=0), hidden_room
    ).reshape(3, 40, 768)
    seconds = [
        jnp.pad(second, ((0, 4), (0, 0)))
        for second in (dino_second, place_columns(siglip_second, siglip_room), sam_second)
    ]
    sums = distil(
        [dino_proj.T, siglip_turned, sam_proj.T, *firsts, *seconds],
        [
            dino_in.reshape(256, -1),
            place_columns(siglip_in.reshape(256, -1), siglip_room),
            sam_in.reshape(1024, -1),
        ],
        student_feats[0],
        mirror_flags((dino_index, siglip_index, sam_index)),
        2.0 / images_total,
    )
    firsts = [total.reshape(40, 32, 24)[..., :20].reshape(40, 640) for total in sums[:3]]
    seconds = [total[:20] for total in sums[3:]]
    siglip_two = seconds[1].reshape(20, 32, 40)[..., :36].reshape(20, 1152)
    return (firsts[0], seconds[0], firsts[1], siglip_two, firsts[2], seconds[2])


def solution(mesh):
    shared = P("wide", None)
    return jax.shard_map(
        body,
        mesh=mesh,
        in_specs=(
            P(("grp", "wide"), None, None),
            *[P("grp", "wide", None)] * 3,
            *[P(None, "wide")] * 3,
            *[P(("grp", "wide"), None)] * 3,
            *[shared] * 6,
        ),
        out_specs=(shared,) * 6,
        check_vma=False,
    )
```

```python
import functools
import itertools
import math

import jax
import jax.numpy as jnp
from jax import lax
from jax.experimental import pallas as pl
from jax.experimental.pallas import tpu as pltpu
from jax.sharding import PartitionSpec as P

MESH = pl.DeviceIdType.MESH
LANE = 128
ALL = (0, 4)
BOTH = (0, 2)


def layer_norm(values, count=None, mask=None):
    count = values.shape[-1] if count is None else count
    centered = values - jnp.sum(values, axis=-1, keepdims=True) * (1.0 / count)
    if mask is not None:
        centered = centered * mask
    variance = jnp.sum(centered * centered, axis=-1, keepdims=True) * (1.0 / count)
    return centered * lax.rsqrt(variance + 1e-05)


def gelu_pair(act):
    cdf = 0.5 * (1.0 + jax.scipy.special.erf(act * (1.0 / math.sqrt(2.0))))
    density = jnp.exp(-0.5 * act * act) * (1.0 / math.sqrt(2.0 * math.pi))
    return (act * cdf, cdf + act * density)


class Place:
    def __init__(self):
        grp, wide = lax.axis_index("grp"), lax.axis_index("wide")
        self.grp, self.wide = grp, wide
        self.z_lo, self.core = grp // 2, grp % 2
        self.y, self.x, self.z_hi = wide // 8, wide // 2 % 4, wide % 2

    def x_next(self, step):
        return (self.grp, (self.y * 4 + self.x_at(step)) * 2 + self.z_hi)

    def y_next(self, step):
        return (self.grp, (self.y_at(step) * 4 + self.x) * 2 + self.z_hi)

    def x_at(self, step):
        return (self.x + step + 4) % 4

    def y_at(self, step):
        return (self.y + step + 4) % 4

    def mirror_z(self):
        return ((1 - self.z_lo) * 2 + self.core, (self.y * 4 + self.x) * 2 + 1 - self.z_hi)

    def next_z(self):
        return ((1 - self.z_lo) * 2 + self.core, self.wide)

    def sibling(self):
        return (self.z_lo * 2 + 1 - self.core, self.wide)


def enter(partners):
    barrier = pltpu.get_barrier_semaphore()
    for partner in partners:
        pl.semaphore_signal(barrier, inc=1, device_id=partner, device_id_type=MESH)
    pl.semaphore_wait(barrier, len(partners))


def part(entry):
    return pl.ds(entry[0], entry[1]) if isinstance(entry, tuple) else entry


def extent(entry):
    return entry[1] if isinstance(entry, tuple) else None


class Copies:
    def __init__(self, send_sem, recv_sem):
        self.send_sem, self.recv_sem = send_sem, recv_sem
        self.started = []

    def send(self, src, dst, device):
        i = len(self.started)
        if i >= SENDS:
            self.started[i - SENDS].wait_send()
        copy = pltpu.make_async_remote_copy(
            src_ref=src,
            dst_ref=dst,
            send_sem=self.send_sem.at[i % SENDS],
            recv_sem=self.recv_sem.at[i],
            device_id=device,
            device_id_type=MESH,
        )
        copy.start()
        self.started.append(copy)
        return copy

    def finish(self):
        for copy in self.started[-SENDS:]:
            copy.wait_send()


class Task:
    def __init__(self, link, cost, needs, run, rank=0):
        self.link, self.cost, self.run, self.rank = link, cost, run, rank
        self.needs = [need for need in needs if need is not None]
        self.copy, self.landed, self.done = None, False, None


BACKLOG = 2.0
LATENCY = 3.0
RATES = {"sibling": 0.4, "local": 0.65}


def span(task):
    return task.cost if task.link == "core" else task.cost * 1e-6 / RATES.get(task.link, 0.0445)


def plan(tasks):
    tails = {id(task): 0.0 for task in tasks}
    for task in reversed(tasks):
        tail = tails[id(task)] + span(task) + (0.0 if task.link == "core" else 1.5)
        for need in task.needs:
            tails[id(need)] = max(tails[id(need)], tail)
    free, now, order, left = {}, 0.0, [], list(tasks)
    while left:
        best = None
        for task in left:
            ready = 0.0
            for need in task.needs:
                if need.done is None:
                    break
                ready = max(ready, need.done)
            else:
                if task.link != "core":
                    ready = max(ready, free.get(task.link, 0.0) - BACKLOG)
                key = (max(ready, now), task.link == "core", task.rank, -tails[id(task)])
                if best is None or key < best[0]:
                    best = (key, task)
        (now, *_), task = best
        if task.link == "core":
            now += task.cost
            task.done = now
        else:
            now += 0.03
            free[task.link] = max(now, free.get(task.link, 0.0)) + span(task)
            task.done = free[task.link] + LATENCY
        order.append(task)
        left.remove(task)
    return order


def carry_out(order):
    for task in order:
        for need in task.needs:
            land(need)
        task.copy = task.run()
    for task in order:
        land(task)


def land(task):
    if task.copy is not None and not task.landed:
        if task.link == "local":
            task.copy.wait()
        else:
            task.copy.wait_recv()
        task.landed = True


WIDTHS = (1536, 1280, 1280)
STUDENT = 1280 + LANE
PROJ_SPLITS = ((2, 1, 2, 1), (1, 2, 1, 1), (1, 1, 1, 2))
FIRST_SPLITS = ((1, 1, 1, 0), (1, 1, 0, 1), (1, 0, 1, 1))
SECOND_SPLITS = ((1, 2, 1, 2), (1, 1, 2, 1), (1, 2, 1, 1))
GRAD_SPLITS = (
    ((1, 0, 1, 1), (0, 1, 1, 1), (1, 1, 1, 0)),
    ((1, 1, 2, 2), (1, 1, 1, 2), (1, 1, 2, 1)),
)
COPIES = 646
SENDS = 48
ORDER = (2, 0, 1)
EARLY = 1
LOCALS = 24


def cut_y(region, half):
    return ((half * 2, 2), region[1], region[2])


def cut_x(region, half):
    return (region[0], (half * 2, 2), region[2])


def cut_z(region, half):
    return (region[0], region[1], half)


def chunks(region):
    return math.prod(extent(entry) or 1 for entry in region)


class Refs:
    def __init__(self, refs):
        self.refs = list(refs)

    def take(self, count):
        taken, self.refs = self.refs[:count], self.refs[count:]
        return taken


def mirror_flags(indices):
    patch = lax.broadcasted_iota(jnp.int32, (8, 256), 1)
    teacher = lax.broadcasted_iota(jnp.int32, (8, 256), 0)
    flags = jnp.zeros((8, 256), jnp.float32)
    for t, index in enumerate(indices):
        same = (index[...] == patch).astype(jnp.float32)
        flags = jnp.where(teacher == t, same, flags)
    row = lax.broadcasted_iota(jnp.int32, (8, LANE), 0)
    lane = lax.broadcasted_iota(jnp.int32, (8, LANE), 1)
    turned = lax.dot_general(
        flags.astype(jnp.bfloat16),
        (row == lane).astype(jnp.bfloat16),
        (((0,), (0,)), ((), ())),
        preferred_element_type=jnp.float32,
    )
    return turned.astype(jnp.bfloat16)


def kernel(factor, *refs):
    refs = Refs(refs)
    shards, inputs, (feats, *indices) = refs.take(9), refs.take(3), refs.take(4)
    outs, weights = refs.take(6), refs.take(6)
    hop_y, ((rows_y,), hop_x, (rows_all,), hop_z) = refs.take(2), (
        refs.take(1),
        refs.take(2),
        refs.take(1),
        refs.take(2),
    )
    projs, (first_all, second_all, rows_in) = refs.take(3), refs.take(3)
    whole = projs + weights
    held, targets = refs.take(3), refs.take(3)
    (act, pred, slope) = refs.take(3)
    normed, normed_too, hidden, hidden_too = (refs.take(3) for _ in range(4))
    grad_act, grad_act_too, grad_pred, grad_pred_too = (refs.take(3) for _ in range(4))
    cells = grad_pred[2]
    sums, last = refs.take(6), refs.take(6)
    (student_in,) = refs.take(1)
    spare, (local_sem, send_sem, recv_sem) = iter(refs.refs[:-3]), refs.refs[-3:]
    at = Place()
    student_in[:, :, :, :1280] = (
        layer_norm(feats[...].astype(jnp.float32))
        .astype(jnp.bfloat16)
        .reshape(4, 4, 16, 1280)
    )
    student_in[:, :, :, 1280:] = mirror_flags(indices).reshape(4, 4, 16, LANE)
    enter(
        [
            at.x_next(1),
            at.x_next(-1),
            at.y_next(1),
            at.y_next(-1),
            at.mirror_z(),
            at.next_z(),
            at.sibling(),
        ]
    )
    copies = Copies(send_sem, recv_sem)
    locals_used = itertools.count()
    tasks = []
    own = (at.y, at.x, at.z_hi)

    def add_task(*args):
        tasks.append(Task(*args))
        return tasks[-1]

    def size_of(ref):
        return math.prod(ref.shape) * 2

    def move(src, dst, needs, rank):
        def run():
            copy = pltpu.make_async_copy(src, dst, local_sem.at[next(locals_used)])
            copy.start()
            return copy

        return add_task("local", size_of(dst), needs, run, rank)

    def carry(src, dst, link, device, needs, rank):
        def run():
            return copies.send(src, dst, device)

        return add_task(link, size_of(dst), needs, run, rank)

    def spread_student():
        x_low, x_high = pl.ds(0, 2), pl.ds(2, 2)
        here = move(student_in.at[at.y], rows_y.at[at.y], [], EARLY)
        got = [here]
        got.append(
            carry(student_in.at[at.y_at(1)], rows_y.at[at.y], "y+", at.y_next(1), [], EARLY)
        )
        got.append(
            carry(student_in.at[at.y_at(-1)], rows_y.at[at.y], "y-", at.y_next(-1), [], EARLY)
        )
        far = student_in.at[at.y_at(2)]
        up = carry(far.at[x_low], hop_y[0], "y+", at.y_next(1), [], EARLY)
        down = carry(far.at[x_high], hop_y[1], "y-", at.y_next(-1), [], EARLY)
        got.append(
            carry(hop_y[0], rows_y.at[at.y_at(-1), x_low], "y+", at.y_next(1), [up], EARLY)
        )
        got.append(
            carry(hop_y[1], rows_y.at[at.y_at(1), x_high], "y-", at.y_next(-1), [down], EARLY)
        )

        every, low, high = pl.ds(0, 4), pl.ds(0, 2), pl.ds(2, 2)
        mine = rows_all.at[every, at.x, at.z_hi]
        done = [move(rows_y.at[every, at.x], mine, got, EARLY)]
        for step, link in ((1, "x+"), (-1, "x-")):
            src = rows_y.at[every, at.x_at(step)]
            done.append(carry(src, mine, link, at.x_next(step), got, EARLY))
        far = at.x_at(2)
        up = carry(rows_y.at[low, far], hop_x[0], "x+", at.x_next(1), got, EARLY)
        down = carry(rows_y.at[high, far], hop_x[1], "x-", at.x_next(-1), got, EARLY)
        dst = rows_all.at[low, at.x_at(-1), at.z_hi]
        done.append(carry(hop_x[0], dst, "x+", at.x_next(1), [up], EARLY))
        dst = rows_all.at[high, at.x_at(1), at.z_hi]
        done.append(carry(hop_x[1], dst, "x-", at.x_next(-1), [down], EARLY))

        landed = []
        for i in range(2):
            one, two = pl.ds(i, 1), pl.ds(2 + i, 1)
            src = rows_all.at[one, every, at.z_hi]
            first = carry(src, hop_z[0].at[one], "mirror", at.mirror_z(), done, EARLY)
            src = rows_all.at[two, every, at.z_hi]
            second = carry(src, hop_z[1].at[one], "next", at.next_z(), done, EARLY)
            dst = rows_all.at[one, every, 1 - at.z_hi]
            src = hop_z[0].at[one]
            landed.append(carry(src, dst, "next", at.next_z(), [first], EARLY))
            dst = rows_all.at[two, every, at.z_hi]
            src = hop_z[1].at[one]
            landed.append(carry(src, dst, "mirror", at.mirror_z(), [second], EARLY))
        return move(rows_all, rows_in, done + landed, EARLY)

    def gather(k, splits, rank):
        shard, array = shards[k], whole[k]
        found = []

        def lanes(s):
            start = at.core * sum(splits) + sum(splits[:s])
            return pl.ds(pl.multiple_of(start * LANE, LANE), splits[s] * LANE)

        def view(s, region):
            return array.at[part(region[0]), part(region[1]), part(region[2]), :, lanes(s)]

        def send(s, region, link, device, needs):
            src = shard.at[:, lanes(s)] if region is own else view(s, region)
            return carry(src, view(s, region), link, device, needs, rank)

        def share(s, region, needs):
            found.append(send(s, region, "sibling", at.sibling(), needs))

        def across(s):
            return [kept, send(s, own, "mirror", at.mirror_z(), [])]

        def across_both(s, needs):
            mine, other = (2 * at.z_lo, 2), (2 - 2 * at.z_lo, 2)
            share(s, (ALL, ALL, at.z_hi), needs)
            one = send(s, (other, ALL, at.z_hi), "mirror", at.mirror_z(), needs)
            two = send(s, (mine, ALL, 1 - at.z_hi), "next", at.next_z(), [one])
            share(s, (mine, ALL, 1 - at.z_hi), [one])
            share(s, (other, ALL, 1 - at.z_hi), [two])
            found.extend(needs + [one, two])

        def last_around(s, axis, block, cut, needs):
            place = at.x_at if axis == "x" else at.y_at
            share(s, block(place(0)), needs)
            up, down, one, two = around(s, axis, block, cut, needs)[len(needs) :]
            share(s, block(place(-1)), [up])
            share(s, block(place(1)), [down])
            share(s, block(place(2)), [one, two])
            found.extend(needs + [up, down, one, two])

        def around(s, axis, block, cut, needs):
            place, device = (at.x_at, at.x_next) if axis == "x" else (at.y_at, at.y_next)
            here = own if cut is None else block(place(0))
            back, ahead = block(place(-1)), block(place(1))
            up = send(s, here, axis + "+", device(1), needs)
            down = send(s, here, axis + "-", device(-1), needs)
            got = needs + [up, down]
            if cut is not None:
                got.append(send(s, cut(back, 0), axis + "+", device(1), [up]))
                got.append(send(s, cut(ahead, 1), axis + "-", device(-1), [down]))
            elif k % 2 == 0:
                got.append(send(s, back, axis + "+", device(1), [up]))
            else:
                got.append(send(s, ahead, axis + "-", device(-1), [down]))
            return got

        def keep():
            start = pl.multiple_of(at.core * sum(splits) * LANE, LANE)
            columns = pl.ds(start, sum(splits) * LANE)
            return move(shard.at[:, columns], array.at[own + (slice(None), columns)], [], -1)

        kept = keep()
        found.append(kept)
        if splits[0]:
            got = around(0, "y", lambda c: (c, at.x, BOTH), cut_z, across(0))
            last_around(0, "x", lambda c: (ALL, c, BOTH), cut_y, got)
        if splits[1]:
            got = around(1, "x", lambda c: (at.y, c, BOTH), cut_z, across(1))
            last_around(1, "y", lambda c: (c, ALL, BOTH), cut_x, got)
        if splits[2]:
            got = [kept] + around(2, "x", lambda c: (at.y, c, at.z_hi), None, [])
            got = around(2, "y", lambda c: (c, ALL, at.z_hi), cut_x, got)
            across_both(2, got)
        if splits[3]:
            got = [kept] + around(3, "y", lambda c: (c, at.x, at.z_hi), None, [])
            got = around(3, "x", lambda c: (ALL, c, at.z_hi), cut_y, got)
            across_both(3, got)
        return found

    def mix(rows_ref, begin, weights, count, mask, write):
        rows = rows_ref[begin : begin + 256, :]
        width = rows.shape[1]
        step = width // 2
        for half in range(2):
            block = weights[2 * half : 2 * half + 2]
            mixed = lax.dot_general(
                rows,
                block.reshape(step, width),
                (((1,), (1,)), ((), ())),
                preferred_element_type=jnp.float32,
            )
            side = rows[:, half * step : (half + 1) * step].astype(jnp.float32)
            pred[:, half * step : (half + 1) * step] = side + mixed

        @pl.loop(0, 2)
        def _(i):
            spot = pl.ds(pl.multiple_of(i * 128, 128), 128)
            values = pred[spot, :width]
            write(spot, layer_norm(values, count, mask).astype(jnp.bfloat16))

    def dino():
        def write(spot, values):
            targets[0][spot, :] = values

        mix(held[0], 0, projs[0], 1536, None, write)

    def siglip():
        def write(spot, values):
            targets[1][spot, :] = values

        column = lax.broadcasted_iota(jnp.int32, (1, 1280), 1)
        mask = (column % 40 < 36).astype(jnp.float32)
        mix(held[1], 0, projs[1], 1152, mask, write)

    def sam(b):
        def run():
            def write(spot, values):
                cells[spot, :] = values

            mix(held[2], b * 256, projs[2], 1280, None, write)
            block = lax.broadcasted_iota(jnp.int32, (64, 256), 0)
            cell = lax.broadcasted_iota(jnp.int32, (64, 256), 1)
            member = ((cell >= 4 * block) & (cell < 4 * block + 4)).astype(jnp.bfloat16)
            total = jnp.dot(member, cells[...], preferred_element_type=jnp.float32)
            targets[2][b * 64 : b * 64 + 64, :] = (total * 0.25).astype(jnp.bfloat16)

        return run

    def pick(t):
        rows = rows_in[...].reshape(512, STUDENT)
        spot = lax.broadcasted_iota(jnp.int32, (256, 512), 0)
        source = lax.broadcasted_iota(jnp.int32, (256, 512), 1)
        column = at.z_hi * 8 + spot % 8
        straight = spot // 8 * 16 + column
        flags = jnp.dot(
            (source == straight).astype(jnp.bfloat16),
            rows[:, 1280:],
            preferred_element_type=jnp.float32,
        )
        shift = jnp.where(flags[:, t : t + 1] > 0.5, 0, 15 - 2 * column)
        normed[t][...] = jnp.dot(
            (source == straight + shift).astype(jnp.bfloat16),
            rows[:, :1280],
            preferred_element_type=jnp.float32,
        ).astype(jnp.bfloat16)

    def forward(t):
        def run():
            pick(t)
            act[...] = jnp.dot(
                normed[t][...],
                first_all[...].reshape(1280, 768),
                preferred_element_type=jnp.float32,
            )

            @pl.loop(0, 8)
            def _(i):
                spot = pl.ds(pl.multiple_of(i * 32, 32), 32)
                hid, tilt = gelu_pair(act[spot, :])
                hidden[t][spot, :] = hid.astype(jnp.bfloat16)
                slope[spot, :] = tilt

        return run

    def backward(t):
        width = WIDTHS[t]

        def run():
            second = second_all[:, :, :, :, :width].reshape(768, width)
            pred[:, :width] = jnp.dot(
                hidden[t][...], second, preferred_element_type=jnp.float32
            )

            @pl.loop(0, 8)
            def _(i):
                spot = pl.ds(pl.multiple_of(i * 32, 32), 32)
                wanted = targets[t][spot, :].astype(jnp.float32)
                grad = factor * (pred[spot, :width] - wanted)
                grad_pred[t][spot, :] = grad.astype(jnp.bfloat16)

            act[...] = lax.dot_general(
                grad_pred[t][...],
                second,
                (((1,), (1,)), ((), ())),
                preferred_element_type=jnp.float32,
            )

            @pl.loop(0, 8)
            def _(i):
                spot = pl.ds(pl.multiple_of(i * 32, 32), 32)
                grad_act[t][spot, :] = (act[spot, :] * slope[spot, :]).astype(jnp.bfloat16)

        return run

    def half_of(width, core):
        return pl.ds(pl.multiple_of(core * (width // 2), LANE), width // 2)

    def outer(left, right):
        return lax.dot_general(
            left, right, (((0,), (0,)), ((), ())), preferred_element_type=jnp.float32
        )

    def gradient(out, left, left_too, right, right_too):
        def run():
            mine, other = right[:, half_of(right.shape[1], at.core)], right_too[...]
            step = left.shape[1] // 2
            for side in range(2):
                columns = slice(step * side, step * side + step)
                total = outer(left[:, columns], mine) + outer(left_too[:, columns], other)
                out[2 * side : 2 * side + 2] = total.reshape((2,) + out.shape[1:])

        return run

    def reduce(k, splits, needs, rank):
        array = sums[k]
        depth = array.shape[3]

        def lanes(s):
            return pl.ds(sum(splits[:s]) * LANE, splits[s] * LANE)

        def view(s, region):
            return array.at[part(region[0]), part(region[1]), part(region[2]), :, lanes(s)]

        def send(s, region, link, device, needs):
            room = next(spare)

            def run():
                return copies.send(view(s, region), room, device)

            size = chunks(region) * depth * splits[s] * LANE * 4
            task = add_task(link, size, needs, run, rank)
            task.room = room
            return task

        def add(s, region, sent, needs):
            sizes = [extent(entry) for entry in region]

            def run():
                for spots in itertools.product(*[range(size or 1) for size in sizes]):
                    there = tuple(spot for spot, size in zip(spots, sizes) if size)
                    where = tuple(
                        spot + entry[0] if size else entry
                        for spot, size, entry in zip(spots, sizes, region)
                    ) + (slice(None), lanes(s))
                    total = array[where]
                    for task in sent:
                        total = total + task.room[there + (slice(None), slice(None))]
                    array[where] = total

            size = chunks(region) * depth * splits[s] * LANE * 4
            return add_task("core", 0.03 + size * 0.06e-6, sent + needs, run, -1)

        def across(s, needs):
            sent = send(s, (at.y, at.x, 1 - at.z_hi), "mirror", at.mirror_z(), needs)
            return [add(s, own, [sent], needs)]

        def across_both(s, needs):
            mine, other = (2 * at.z_lo, 2), (2 - 2 * at.z_lo, 2)
            sent = send(s, (other, ALL, 1 - at.z_hi), "next", at.next_z(), needs)
            added = add(s, (mine, ALL, 1 - at.z_hi), [sent], needs)
            sent = send(s, (mine, ALL, 1 - at.z_hi), "mirror", at.mirror_z(), [added])
            return [add(s, (other, ALL, at.z_hi), [sent], needs)]

        def around(s, axis, block, cut, needs):
            place, device = (at.x_at, at.x_next) if axis == "x" else (at.y_at, at.y_next)
            here, over, back, ahead = (block(place(step)) for step in (0, 2, -1, 1))
            up, down = [], []
            if cut is not None:
                sent = send(s, cut(over, 0), axis + "+", device(1), needs)
                up.append(add(s, cut(ahead, 0), [sent], needs))
                sent = send(s, cut(over, 1), axis + "-", device(-1), needs)
                down.append(add(s, cut(back, 1), [sent], needs))
            elif k % 2 == 0:
                sent = send(s, over, axis + "+", device(1), needs)
                up.append(add(s, ahead, [sent], needs))
            else:
                sent = send(s, over, axis + "-", device(-1), needs)
                down.append(add(s, back, [sent], needs))
            one = send(s, ahead, axis + "+", device(1), needs + up)
            two = send(s, back, axis + "-", device(-1), needs + down)
            return [add(s, here, [one, two], needs)]

        def settle(needs):
            mine = half_of(outs[k].shape[1], at.core)

            def swap():
                return copies.send(array.at[own], last[k], at.next_z())

            def total():
                outs[k][:, mine] = array[own] + last[k][...]

            def share_total():
                return copies.send(outs[k].at[:, mine], outs[k].at[:, mine], at.sibling())

            size = depth * sum(splits) * LANE * 4
            swapped = add_task("next", size, needs, swap, -1)
            added = add_task("core", 0.1, needs + [swapped], total, -1)
            add_task("sibling", size, [added], share_total, -1)

        done = []
        if splits[0]:
            got = around(0, "x", lambda c: (ALL, c, BOTH), cut_y, needs)
            got = around(0, "y", lambda c: (c, at.x, BOTH), cut_z, got)
            done += across(0, got)
        if splits[1]:
            got = around(1, "y", lambda c: (c, ALL, BOTH), cut_x, needs)
            got = around(1, "x", lambda c: (at.y, c, BOTH), cut_z, got)
            done += across(1, got)
        if splits[2]:
            got = across_both(2, needs)
            got = around(2, "y", lambda c: (c, ALL, at.z_hi), cut_x, got)
            done += around(2, "x", lambda c: (at.y, c, at.z_hi), None, got)
        if splits[3]:
            got = across_both(3, needs)
            got = around(3, "x", lambda c: (ALL, c, at.z_hi), cut_y, got)
            done += around(3, "y", lambda c: (c, at.x, at.z_hi), None, got)
        settle(done)

    loaded = [move(inputs[t], held[t], [], 10 * ORDER.index(t) + 3) for t in range(3)]
    rows_ready = None
    before = None
    for place, t in enumerate(ORDER):
        rank = 10 * place
        projected = gather(t, PROJ_SPLITS[t], rank)
        needs = projected + [loaded[t]]
        if t == 0:
            mapped = [add_task("core", 2.0, needs, dino, rank + 1)]
        elif t == 1:
            mapped = [add_task("core", 1.7, needs, siglip, rank + 1)]
        else:
            mapped = [add_task("core", 1.8, needs, sam(b), rank + 1) for b in range(4)]
        if rows_ready is None:
            rows_ready = spread_student()
        first = gather(3 + t, FIRST_SPLITS[t], rank + 1)
        second = gather(6 + t, SECOND_SPLITS[t], rank + 2)
        free = [before] if before else []
        ahead = [forwarded] if before else []
        first = move(whole[3 + t], first_all, first + ahead, rank)
        second = move(
            whole[6 + t], second_all.at[:, :, :, :, pl.ds(0, WIDTHS[t])], second + free, rank
        )
        forwarded = add_task("core", 2.1, [rows_ready, first] + free, forward(t), rank + 3)

        def share(src, dst, needs, rank=rank):
            if src.shape[1] != dst.shape[1]:
                src = src.at[:, half_of(src.shape[1], 1 - at.core)]
            return carry(src, dst, "sibling", at.sibling(), needs, rank)

        got_normed = share(normed[t], normed_too[t], [forwarded])
        got_hidden = share(hidden[t], hidden_too[t], [forwarded])
        before = add_task("core", 2.1, [second, forwarded] + mapped, backward(t), rank + 3)
        got_act = share(grad_act[t], grad_act_too[t], [before])
        got_pred = share(grad_pred[t], grad_pred_too[t], [before])
        run = gradient(sums[t], normed[t], normed_too[t], grad_act[t], grad_act_too[t])
        done = add_task("core", 0.6, [before, got_normed, got_act], run, rank + 2)
        reduce(t, GRAD_SPLITS[0][t], [done], 40 + place)
        run = gradient(sums[3 + t], hidden[t], hidden_too[t], grad_pred[t], grad_pred_too[t])
        done = add_task("core", 0.7, [before, got_hidden, got_pred], run, rank + 2)
        reduce(3 + t, GRAD_SPLITS[1][t], [done], 40 + place)
    carry_out(plan(tasks))
    copies.finish()


def distil(shards, inputs, feats, indices, factor):
    inside = pl.BlockSpec(memory_space=pltpu.VMEM)
    outside = pl.BlockSpec(memory_space=pl.ANY)
    depth = [40] * 3 + [24] * 3
    width = [384] * 3 + [w // 2 for w in WIDTHS]
    splits = GRAD_SPLITS[0] + GRAD_SPLITS[1]

    def rooms():
        plane, line = [(2, 2), (2, 2), (4, 2), (4, 2)], [(), (), (2,), (2,)]
        column, spot = [(2,), (2,), (4,), (4,)], [(), (), ()]
        leads = [plane + line + [()]] * 2 + [[(2, 4), (2, 4)] + column + spot] * 2
        for t in ORDER:
            for k in (t, 3 + t):
                for s in range(4):
                    if splits[k][s]:
                        for lead in leads[s]:
                            yield pltpu.VMEM(lead + (depth[k], splits[k][s] * LANE), jnp.float32)

    def half_wide(*shape):
        return jax.ShapeDtypeStruct(shape, jnp.bfloat16)

    def table(*shape):
        return pltpu.VMEM(shape, jnp.bfloat16)

    def three(*widths):
        return [table(256, w) for w in widths]

    outs = [jax.ShapeDtypeStruct((d, 2 * w), jnp.float32) for d, w in zip(depth, width)]
    landings = [half_wide(4, 4, 2, *shard.shape) for shard in shards[3:]] + [
        half_wide(2, 16, STUDENT),
        half_wide(2, 16, STUDENT),
        half_wide(4, 4, 16, STUDENT),
        half_wide(2, 16, STUDENT),
        half_wide(2, 16, STUDENT),
        half_wide(4, 4, 2, 16, STUDENT),
        half_wide(2, 4, 16, STUDENT),
        half_wide(2, 4, 16, STUDENT),
    ]
    results = pl.pallas_call(
        functools.partial(kernel, factor),
        out_shape=outs + landings,
        in_specs=[outside] * (len(shards) + len(inputs)) + [inside] * 4,
        out_specs=[inside] * len(outs) + [outside] * len(landings),
        scratch_shapes=[
            table(4, 4, 2, 48, 1536),
            table(4, 4, 2, 40, 1280),
            table(4, 4, 2, 40, 1280),
            table(4, 4, 2, 40, 768),
            table(4, 4, 2, 24, 1536),
            table(4, 4, 2, 16, STUDENT),
            *[table(*rows.shape) for rows in inputs],
            *three(*WIDTHS),
            pltpu.VMEM((256, 768), jnp.float32),
            pltpu.VMEM((256, 1536), jnp.float32),
            pltpu.VMEM((256, 768), jnp.float32),
            *three(*[1280] * 6),
            *three(*[768] * 6),
            *three(*[768] * 3),
            *three(*[384] * 3),
            *three(*WIDTHS),
            *three(*[w // 2 for w in WIDTHS]),
            *[pltpu.VMEM((4, 4, 2, d, w), jnp.float32) for d, w in zip(depth, width)],
            *[pltpu.VMEM((d, w), jnp.float32) for d, w in zip(depth, width)],
            table(4, 4, 16, STUDENT),
            *rooms(),
            pltpu.SemaphoreType.DMA((LOCALS,)),
            pltpu.SemaphoreType.DMA((SENDS,)),
            pltpu.SemaphoreType.DMA((COPIES,)),
        ],
        compiler_params=pltpu.CompilerParams(
            collective_id=0, has_side_effects=True, vmem_limit_bytes=63 * 1024 * 1024
        ),
        name="distil",
    )(*shards, *inputs, feats, *indices)
    return results[: len(outs)]


def spread(width, group, room):
    rows = lax.broadcasted_iota(jnp.int32, (width, width // group * room), 0)
    columns = lax.broadcasted_iota(jnp.int32, (width, width // group * room), 1)
    return (rows // group * room + rows % group == columns).astype(jnp.bfloat16)


def place_columns(values, table):
    return jnp.dot(values, table, preferred_element_type=jnp.float32).astype(jnp.bfloat16)


def body(
    student_feats,
    dino_in,
    siglip_in,
    sam_in,
    dino_proj,
    siglip_proj,
    sam_proj,
    dino_index,
    siglip_index,
    sam_index,
    dino_first,
    dino_second,
    siglip_first,
    siglip_second,
    sam_first,
    sam_second,
):
    images_total = student_feats.shape[0] * 128
    siglip_room = spread(1152, 36, 40)
    hidden_room = spread(640, 20, 24)
    siglip_turned = jnp.pad(place_columns(siglip_proj.T, siglip_room), ((0, 4), (0, 0)))
    firsts = place_columns(
        jnp.concatenate([dino_first, siglip_first, sam_first], axis=0), hidden_room
    ).reshape(3, 40, 768)
    seconds = [
        jnp.pad(second, ((0, 4), (0, 0)))
        for second in (dino_second, place_columns(siglip_second, siglip_room), sam_second)
    ]
    sums = distil(
        [dino_proj.T, siglip_turned, sam_proj.T, *firsts, *seconds],
        [
            dino_in.reshape(256, -1),
            place_columns(siglip_in.reshape(256, -1), siglip_room),
            sam_in.reshape(1024, -1),
        ],
        student_feats[0],
        (dino_index, siglip_index, sam_index),
        2.0 / images_total,
    )
    firsts = [total.reshape(40, 32, 24)[..., :20].reshape(40, 640) for total in sums[:3]]
    seconds = [total[:20] for total in sums[3:]]
    siglip_two = seconds[1].reshape(20, 32, 40)[..., :36].reshape(20, 1152)
    return (firsts[0], seconds[0], firsts[1], siglip_two, firsts[2], seconds[2])


def solution(mesh):
    shared = P("wide", None)
    return jax.shard_map(
        body,
        mesh=mesh,
        in_specs=(
            P(("grp", "wide"), None, None),
            *[P("grp", "wide", None)] * 3,
            *[P(None, "wide")] * 3,
            *[P(("grp", "wide"), None)] * 3,
            *[shared] * 6,
        ),
        out_specs=(shared,) * 6,
        check_vma=False,
    )
```
